128 devices in a mesh: rows: 16 (over x_lo, z, core), cols: 8 (over x_hi, y).
Axes of the slice: x: 4 (x_hi: 2, x_lo: 2; x = x_hi * 2 + x_lo), y: 4, z: 4, core: 2. Of those that a mesh axis runs over, the one named last changes fastest.
Arguments:
- image: bfloat16 [256, 128, 1024], P('rows', 'cols'), may hold values from -6 to 6
- gain_conv: float32 [1024], replicated, may hold values from 0.1 to 1.9
- w_expand: bfloat16 [1024, 4096], replicated, may hold values from -0.1875 to 0.1875
- kernel: float32 [3, 3, 4096], replicated, may hold values from -2 to 2
- w_project: bfloat16 [4096, 1024], replicated, may hold values from -0.09375 to 0.09375
- gain_attn: float32 [1024], replicated, may hold values from 0.1 to 1.9
- w_qkv: bfloat16 [1024, 3072], replicated, may hold values from -0.1875 to 0.1875
- bias_table: float32 [32, 15, 15], replicated, may hold values from -3.5 to 310
- w_out: bfloat16 [1024, 1024], replicated, may hold values from -0.1875 to 0.1875
- cotangent: bfloat16 [256, 128, 1024], P('rows', 'cols'), may hold values from -6 to 6
Outputs:
- output_map: bfloat16 [256, 128, 1024], P('rows', 'cols')
- d_image: bfloat16 [256, 128, 1024], P('rows', 'cols')
The draws below stay inside these ranges and needn't reach their ends.
All inputs are finite; a program needn't handle non-finite values.
Results may differ from the reference program's by a relative error of at most 0.022.
Values may be sent and summed in bfloat16 or wider, within the bound.
A program may use at most 128 MiB of HBM per device.

```python
import jax
import jax.numpy as jnp
from jax import lax

D = 1024
HEADS = 32
E = 4096
GRID = 8
TABLE = 15
NH = 256
NW = 128


def draw_bias_table(key, part):
    key = jax.random.fold_in(key, 11)
    return jnp.clip(jax.random.normal(key, (HEADS, TABLE, TABLE), jnp.float32), -3.5, 3.5)


def steps_of(key, shape, split, least, high):
    def one(dim, blocks):
        draws = jax.random.uniform(jax.random.fold_in(jax.random.fold_in(key, 6), dim), (blocks,), jnp.float32, least / len(split), high / len(split))
        return jnp.repeat(jnp.exp(draws), shape[dim] // blocks).reshape((-1,) + (1,) * (len(shape) - dim - 1))

    factor_of = one(*split[0])
    for cut in split[1:]:
        factor_of = factor_of * one(*cut)
    return factor_of


def normal_values(key, dims, width, limit, cuts=(), held_as=jnp.bfloat16):
    drawn = jax.random.normal(key, dims, jnp.float32) * width
    if len(cuts) > 0:
        drawn = steps_of(key, dims, cuts, -0.22, 0.18) * drawn
    return jnp.clip(drawn, min=-limit, max=limit).astype(held_as)


def setup_inputs(seed: int = 0) -> dict:
    seeds = jax.random.split(jax.random.key(seed), 11)
    return {
        "image": normal_values(seeds[0], (NH, NW, D), 1.0, 6.0, ((0, 16), (1, 8))),
        "gain_conv": jnp.clip(1.0 + 0.18 * jax.random.normal(seeds[1], (D,), jnp.float32), 0.1, 1.9),
        "w_expand": normal_values(seeds[2], (D, E), D ** -0.5, 0.1875),
        "kernel": normal_values(seeds[3], (3, 3, E), 9 ** -0.5, 2.0, (), jnp.float32),
        "w_project": normal_values(seeds[4], (E, D), E ** -0.5, 0.09375),
        "gain_attn": jnp.clip(1.0 + 0.18 * jax.random.normal(seeds[5], (D,), jnp.float32), 0.1, 1.9),
        "w_qkv": normal_values(seeds[6], (D, 3 * D), D ** -0.5, 0.1875),
        "bias_table": draw_bias_table(jax.random.fold_in(seeds[10], 71), 0),
        "w_out": normal_values(seeds[8], (D, D), D ** -0.5, 0.1875),
        "cotangent": normal_values(seeds[9], (NH, NW, D), 1.0, 6.0, ((0, 16), (1, 8))),
    }


epsilon = 1e-05

def normalize(inputs, gain_vector):
    values = inputs.astype(jnp.float32)
    centered = values - lax.optimization_barrier(jnp.mean(values, axis=-1, keepdims=True))
    spread = lax.optimization_barrier(jnp.mean(centered * centered, axis=-1, keepdims=True))
    return (centered * lax.rsqrt(spread + epsilon) * gain_vector).astype(jnp.bfloat16)

def activate(values):
    return jax.nn.gelu(values, approximate=False)

def expand_cells(normed, w_expand):
    before = jnp.dot(normed, w_expand, preferred_element_type=jnp.float32)
    return (activate(before).astype(jnp.bfloat16), before)

def expand_back(d_widened, before, w_expand):
    _, slope_back = jax.vjp(activate, before)
    d_before = slope_back(d_widened.astype(jnp.float32))[0].astype(jnp.bfloat16)
    return jnp.einsum('rcf,df->rcd', d_before, w_expand, preferred_element_type=jnp.float32).astype(jnp.bfloat16)

def depthwise(padded, kernel):
    height = padded.shape[0] - 2
    breadth = padded.shape[1] - 2
    running = jnp.zeros((height, breadth, padded.shape[2]), jnp.float32)
    for shift_row in range(3):
        for shift_col in range(3):
            window = padded[shift_row:shift_row + height, shift_col:shift_col + breadth].astype(jnp.float32)
            running = running + window * kernel[shift_row, shift_col]
    return running

def conv_residual(residual_in, branch_in, w_project):
    return (residual_in.astype(jnp.float32) + jnp.dot(branch_in, w_project, preferred_element_type=jnp.float32)).astype(jnp.bfloat16)

def project(normed, w_qkv):
    return jnp.dot(normed, w_qkv, preferred_element_type=jnp.float32).astype(jnp.bfloat16)

def finish(residual_in, branch_in, w_out):
    return residual_in.astype(jnp.float32) + jnp.dot(branch_in, w_out, preferred_element_type=jnp.float32)

def relative_bias(bias_table):
    head_count = bias_table.shape[0]
    member = jnp.arange(GRID * GRID)
    member_row = member // GRID
    member_col = member % GRID
    offset = (member_row[:, None] - member_row[None, :] + GRID - 1) * (2 * GRID - 1) + (member_col[:, None] - member_col[None, :] + GRID - 1)
    onehot = (offset[:, :, None] == jnp.arange((2 * GRID - 1) ** 2)[None, None, :]).astype(jnp.float32)
    return jnp.einsum('qkt,ht->hqk', onehot, bias_table.reshape(head_count, -1), precision=lax.Precision.HIGHEST)

def attend(grouped, bias_full):
    groups, members, triple = grouped.shape
    model_width = triple // 3
    head_count = bias_full.shape[0]
    head_size = model_width // head_count
    pieces = grouped.reshape(groups, members, 3, head_count, head_size)
    query_part = pieces[:, :, 0]
    key_part = pieces[:, :, 1]
    value_part = pieces[:, :, 2]
    scores = jnp.einsum('gqhd,gkhd->ghqk', query_part, key_part, preferred_element_type=jnp.float32)
    scores = scores * head_size ** (-0.5) + bias_full[None]
    attention_weights = jax.nn.softmax(scores, axis=-1).astype(jnp.bfloat16)
    weighted = jnp.einsum('ghqk,gkhd->gqhd', attention_weights, value_part, preferred_element_type=jnp.float32)
    return weighted.reshape(groups, members, model_width).astype(jnp.bfloat16)

def to_grid(field):
    height, breadth, features = field.shape
    band_rows = height // GRID
    band_cols = breadth // GRID
    shaped = field.reshape(GRID, band_rows, GRID, band_cols, features).transpose(1, 3, 0, 2, 4)
    return shaped.reshape(band_rows * band_cols, GRID * GRID, features)

def from_grid(grouped, height, breadth):
    features = grouped.shape[-1]
    band_rows = height // GRID
    band_cols = breadth // GRID
    shaped = grouped.reshape(band_rows, band_cols, GRID, GRID, features).transpose(2, 0, 3, 1, 4)
    return shaped.reshape(height, breadth, features)

def reference(image, gain_conv, w_expand, kernel, w_project, gain_attn, w_qkv, bias_table, w_out, cotangent):
    height = image.shape[0]
    breadth = image.shape[1]
    padding = ((1, 1), (1, 1), (0, 0))
    bias_full = relative_bias(bias_table)
    normed_in, norm_back = jax.vjp(lambda inputs: normalize(inputs, gain_conv), image)
    widened, before = expand_cells(normed_in, w_expand)
    conv_sum = depthwise(jnp.pad(widened, padding), kernel)
    activated, activate_back = jax.vjp(lambda inputs: activate(inputs).astype(jnp.bfloat16), conv_sum)
    merged, residual_back = jax.vjp(lambda residual_in, branch_in: conv_residual(residual_in, branch_in, w_project), image, activated)
    qkv_map, qkv_back = jax.vjp(lambda inputs: project(normalize(inputs, gain_attn), w_qkv), merged)
    attended, attend_back = jax.vjp(lambda inputs: attend(inputs, bias_full), to_grid(qkv_map))
    result, finish_back = jax.vjp(lambda residual_in, branch_in: finish(residual_in, branch_in, w_out), merged, from_grid(attended, height, breadth))
    d_merged_a, d_attended = finish_back(cotangent.astype(jnp.float32))
    d_grouped = attend_back(to_grid(d_attended))[0]
    d_merged_b = qkv_back(from_grid(d_grouped, height, breadth))[0]
    d_merged = (d_merged_a.astype(jnp.float32) + d_merged_b.astype(jnp.float32)).astype(jnp.bfloat16)
    d_image_a, d_activated = residual_back(d_merged)
    d_conv = activate_back(d_activated)[0].astype(jnp.bfloat16)
    d_widened = depthwise(jnp.pad(d_conv, padding), kernel[::-1, ::-1]).astype(jnp.bfloat16)
    d_normed = expand_back(d_widened, before, w_expand)
    d_image_b = norm_back(d_normed)[0]
    d_image = (d_image_a.astype(jnp.float32) + d_image_b.astype(jnp.float32)).astype(jnp.bfloat16)
    return (result.astype(jnp.bfloat16), d_image)
```

```python
import jax
import jax.numpy as jnp
from jax import lax
from jax.experimental import pallas as pl
from jax.experimental.pallas import tpu as pltpu
from jax.sharding import PartitionSpec as P

F32 = jnp.float32
BF16 = jnp.bfloat16
MESH = pl.DeviceIdType.MESH
EPS = 1e-05
GRID = 8
T = 256
D = 1024
E = 4096
CH = 512
NCH = E // CH
QCH = 3 * D // CH
NT = (((1,), (1,)), ((), ()))


def dot_nt(a, b):
    return lax.dot_general(a, b, NT, preferred_element_type=F32)


def dot_nn(a, b):
    return jnp.dot(a, b, preferred_element_type=F32)


def gelu_parts(v):
    e = jnp.exp2(v * v * (-0.5 * 1.4426950408889634))
    t = pl.reciprocal(1.0 + jnp.abs(v) * (0.3275911 * 0.7071067811865476))
    poly = t * (0.5 * 1.061405429) + (0.5 * -1.453152027)
    poly = poly * t + (0.5 * 1.421413741)
    poly = poly * t + (0.5 * -0.284496736)
    poly = poly * t + (0.5 * 0.254829592)
    tail = poly * t * e
    cdf = jnp.where(v >= 0, 1.0 - tail, tail)
    return cdf, e * 0.3989422804014327


def kernel(
    img,
    gain_c,
    we,
    kern,
    wp,
    gain_a,
    wqkv,
    table,
    wo,
    cot,
    out,
    dimg,
    we_v,
    wp_v,
    wqkv_v,
    wo_v,
    wid,
    s1,
    s2,
    hs,
    hr,
    cs,
    csb,
    cr,
    hrf,
    crf,
    before,
    act,
    acc,
    xs,
    ys,
    na,
    send,
    recv,
    cotg,
    mg,
    qkv,
    datt,
    att,
    dqkv,
    wtab,
    btile,
    w_sem,
    hsend_sem,
    hrecv_sem,
    csend_sem,
    crecv_sem,
    asend_sem,
    arecv_sem,
    aown_sem,
):
    nrow = lax.axis_size("rows")
    ncol = lax.axis_size("cols")
    R = lax.axis_index("rows")
    C = lax.axis_index("cols")
    core = lax.rem(R, 2)
    me = (R // 2) * ncol + C
    npeer = (nrow // 2) * ncol

    def we_copy(k):
        return pltpu.make_async_copy(
            we.at[:, pl.ds(pl.multiple_of(k * CH, CH), CH)], we_v.at[k], w_sem.at[0, k]
        )

    def wp_copy(k):
        return pltpu.make_async_copy(
            wp.at[pl.ds(pl.multiple_of(k * CH, CH), CH), :], wp_v.at[k], w_sem.at[1, k]
        )

    def wqkv_copy(k):
        return pltpu.make_async_copy(
            wqkv.at[:, pl.ds(pl.multiple_of(k * CH, CH), CH)], wqkv_v.at[k], w_sem.at[2, k]
        )

    wo_copy = pltpu.make_async_copy(wo, wo_v, w_sem.at[3, 0])
    for k in range(NCH):
        we_copy(k).start()
    wo_copy.start()
    for k in range(NCH):
        wp_copy(k).start()
    for k in range(QCH):
        wqkv_copy(k).start()

    barrier = pltpu.get_barrier_semaphore()

    def peer_coord(d):
        return (2 * (d // ncol) + core, lax.rem(d, ncol))

    def greet(q, carry):
        pr, pc = peer_coord(lax.rem(me + q, npeer))
        pl.semaphore_signal(barrier, inc=1, device_id=(pr, pc), device_id_type=MESH)
        return carry

    lax.fori_loop(1, npeer, greet, 0)
    has_u = R > 0
    has_d = R < nrow - 1
    has_l = C > 0
    has_r = C < ncol - 1
    for dr, cond_r in ((-1, has_u), (1, has_d)):
        for dc, cond_c in ((-1, has_l), (0, None), (1, has_r)):
            cond = cond_r if cond_c is None else jnp.logical_and(cond_r, cond_c)

            @pl.when(cond)
            def _():
                pl.semaphore_signal(
                    barrier, inc=1, device_id=(R + dr, C + dc), device_id_type=MESH
                )

    sides = ((-1, 0, has_u), (1, 0, has_d), (0, -1, has_l), (0, 1, has_r))
    corners = (
        (-1, -1, jnp.logical_and(has_u, has_l)),
        (-1, 1, jnp.logical_and(has_u, has_r)),
        (1, -1, jnp.logical_and(has_d, has_l)),
        (1, 1, jnp.logical_and(has_d, has_r)),
    )
    for s, (_, _, cond) in enumerate(sides):

        @pl.when(jnp.logical_not(cond))
        def _():
            for way in range(2):
                hr[way, :, s] = jnp.zeros((NCH, 16, CH), BF16)

    for s, (_, _, cond) in enumerate(corners):

        @pl.when(jnp.logical_not(cond))
        def _():
            for way in range(2):
                cr[way, :, s] = jnp.zeros((2, 16, 128), BF16)

    def side_copy(way, k, s):
        dr, dc, _ = sides[s]
        return pltpu.make_async_remote_copy(
            src_ref=hs.at[k, s],
            dst_ref=hr.at[way, k, s ^ 1],
            send_sem=hsend_sem.at[way, k, s],
            recv_sem=hrecv_sem.at[way, k, s ^ 1],
            device_id=(R + dr, C + dc),
            device_id_type=MESH,
        )

    def side_recv(way, k, s):
        return pltpu.make_async_copy(hs.at[k, s], hr.at[way, k, s], hrecv_sem.at[way, k, s])

    def corner_copy(way, half, s):
        dr, dc, _ = corners[s]
        return pltpu.make_async_remote_copy(
            src_ref=csb.at[half, s],
            dst_ref=cr.at[way, half, 3 - s],
            send_sem=csend_sem.at[way, half, s],
            recv_sem=crecv_sem.at[way, half, 3 - s],
            device_id=(R + dr, C + dc),
            device_id_type=MESH,
        )

    def corner_recv(way, half, s):
        return pltpu.make_async_copy(
            csb.at[half, s], cr.at[way, half, s], crecv_sem.at[way, half, s]
        )

    def send_halos(way, k):
        for j in range(CH // 128):
            lanes = slice(128 * j, 128 * j + 128)
            tile = 4 * k + j
            hs[k, 0, :, lanes] = wid[tile, 0:16, :].astype(BF16)
            hs[k, 1, :, lanes] = wid[tile, T - 16 : T, :].astype(BF16)
            hs[k, 2, :, lanes] = wid[tile, pl.ds(0, 16, stride=16), :].astype(BF16)
            hs[k, 3, :, lanes] = wid[tile, pl.ds(15, 16, stride=16), :].astype(BF16)
            for s, row in enumerate((0, 15, T - 16, T - 1)):
                cs[s, pl.ds(tile, 1), :] = wid[tile, row : row + 1, :]
        for s, (_, _, cond) in enumerate(sides):

            @pl.when(cond)
            def _():
                side_copy(way, k, s).start()

        for half in range(2):

            @pl.when(k == 4 * half + 3)
            def _():
                for s, (_, _, cond) in enumerate(corners):
                    csb[half, s] = cs[s, 16 * half : 16 * half + 16, :].astype(BF16)

                    @pl.when(cond)
                    def _():
                        corner_copy(way, half, s).start()

    def wait_halos(way, k):
        for s, (_, _, cond) in enumerate(sides):

            @pl.when(cond)
            def _():
                side_recv(way, k, s).wait()

        for half in range(2):

            @pl.when(k == 4 * half)
            def _():
                for s, (_, _, cond) in enumerate(corners):

                    @pl.when(cond)
                    def _():
                        corner_recv(way, half, s).wait()

                    crf[s, 16 * half : 16 * half + 16, :] = cr[way, half, s].astype(F32)

        for s in range(4):
            hrf[s] = hr[way, k, s].astype(F32)

    def wait_halo_sends(way):
        def one(k, carry):
            for s, (_, _, cond) in enumerate(sides):

                @pl.when(cond)
                def _():
                    side_copy(way, k, s).wait_send()

            return carry

        lax.fori_loop(0, NCH, one, 0)
        for half in range(2):
            for s, (_, _, cond) in enumerate(corners):

                @pl.when(cond)
                def _():
                    corner_copy(way, half, s).wait_send()

    def a2a_start(n):
        def one(q, carry):
            d = lax.rem(me + q, npeer)
            pltpu.make_async_remote_copy(
                src_ref=send.at[n, d],
                dst_ref=recv.at[n, me],
                send_sem=asend_sem.at[n],
                recv_sem=arecv_sem.at[n],
                device_id=peer_coord(d),
                device_id_type=MESH,
            ).start()
            return carry

        lax.fori_loop(1, npeer, one, 0)
        pltpu.make_async_copy(send.at[n, me], recv.at[n, me], aown_sem.at[n]).start()

    def a2a_wait(n):
        part = pl.ds(0, npeer - 1)
        pltpu.make_async_copy(send.at[n, me], recv.at[n, me], aown_sem.at[n]).wait()
        pltpu.make_async_copy(send.at[n, part], recv.at[n, part], arecv_sem.at[n]).wait()

    def a2a_wait_send(n):
        part = pl.ds(0, npeer - 1)
        pltpu.make_async_copy(send.at[n, part], recv.at[n, part], asend_sem.at[n]).wait()

    def pack(n, grouped):
        for b in range(8):
            for t in range(4):
                rows = pl.ds(64 * t, 64) if grouped else pl.ds(t, 64, stride=4)
                ys[pl.ds(4 * b + t, 64, stride=32), :] = xs[b, rows, :]
        send[n] = ys[...].reshape(64, 32, 128).astype(BF16)

    def unpack(n, grouped):
        ys[...] = recv[n].astype(F32).reshape(2048, 128)
        for b in range(8):
            for t in range(4):
                rows = pl.ds(64 * t, 64) if grouped else pl.ds(t, 64, stride=4)
                xs[b, rows, :] = ys[pl.ds(4 * b + t, 64, stride=32), :]

    def put_xs(rows, value):
        for b in range(8):
            xs[b, rows, :] = value[:, 128 * b : 128 * b + 128]

    def get_xs(rows):
        return jnp.concatenate([xs[b, rows, :] for b in range(8)], axis=1)

    def put_wid(k, rows, value):
        for j in range(CH // 128):
            wid[4 * k + j, rows, :] = value[:, 128 * j : 128 * j + 128]

    def tiles(body, size=32):
        def one(i, carry):
            body(pl.ds(pl.multiple_of(i * size, size), size))
            return carry

        lax.fori_loop(0, T // size, one, 0)

    def norm_parts(x):
        c = x - jnp.mean(x, axis=-1, keepdims=True)
        r = lax.rsqrt(jnp.mean(c * c, axis=-1, keepdims=True) + EPS)
        return c * r, r

    def norm_back(x, dy, gain):
        xh, r = norm_parts(x)
        dg = dy * gain
        m1 = jnp.mean(dg, axis=-1, keepdims=True)
        m2 = jnp.mean(dg * xh, axis=-1, keepdims=True)
        return (dg - m1 - xh * m2) * r

    def norm_in(rows):
        xh, _ = norm_parts(img[rows, :].astype(F32))
        na[rows, :] = (xh * gain_c[...]).astype(BF16)
        put_xs(rows, cot[rows, :].astype(F32))

    tiles(norm_in)
    pack(0, False)

    n_other = (has_u.astype(jnp.int32) + has_d.astype(jnp.int32)) * (
        1 + has_l.astype(jnp.int32) + has_r.astype(jnp.int32)
    )
    pl.semaphore_wait(barrier, npeer - 1 + n_other)
    a2a_start(0)

    def expand(k, carry):
        we_copy(k).wait()
        before[...] = dot_nn(na[...], we_v[k])

        def act_tile(rows):
            v = before[rows, :]
            cdf, pdf = gelu_parts(v)
            put_wid(k, rows, v * cdf)
            s1[k, rows, :] = (cdf + v * pdf).astype(BF16)

        tiles(act_tile)
        send_halos(0, k)
        return carry

    lax.fori_loop(0, NCH, expand, 0)

    iota16 = lax.broadcasted_iota(jnp.int32, (16, 128), 0)
    at_first = iota16 == 0
    at_last = iota16 == 15

    def conv(k, j, flip, done):
        lanes = slice(128 * j, 128 * j + 128)
        wide = pl.ds(pl.multiple_of(k * CH + 128 * j, 128), 128)
        w = [
            [kern[2 - a if flip else a, pl.ds(2 - b if flip else b, 1), wide] for b in range(3)]
            for a in range(3)
        ]
        sums = {}
        for r in range(-1, 17):
            if r == -1 or r == 16:
                low = r == 16
                x = hrf[1 if low else 0, :, lanes]
                cell = pl.ds(4 * k + j, 1)
                left = crf[2 if low else 0, cell, :]
                right = crf[3 if low else 1, cell, :]
            else:
                x = wid[4 * k + j, 16 * r : 16 * r + 16, :]
                left = hrf[2, r : r + 1, lanes]
                right = hrf[3, r : r + 1, lanes]
            xl = jnp.where(at_first, left, pltpu.roll(x, 1, 0))
            xr = jnp.where(at_last, right, pltpu.roll(x, 15, 0))
            for a in range(3):
                ro = r - a + 1
                if 0 <= ro < 16:
                    part = xl * w[a][0] + x * w[a][1] + xr * w[a][2]
                    sums[ro] = sums[ro] + part if ro in sums else part
            if r >= 1:
                done(r - 1, sums.pop(r - 1))

    acc[...] = jnp.zeros((T, D), F32)

    def project(k, carry):
        wait_halos(0, k)
        for j in range(CH // 128):
            lanes = slice(128 * j, 128 * j + 128)

            def done(r, v):
                cdf, pdf = gelu_parts(v)
                act[16 * r : 16 * r + 16, lanes] = (v * cdf).astype(BF16)
                s2[k, 16 * r : 16 * r + 16, lanes] = (cdf + v * pdf).astype(BF16)

            conv(k, j, False, done)
        wp_copy(k).wait()
        acc[...] += dot_nn(act[...], wp_v[k])
        return carry

    lax.fori_loop(0, NCH, project, 0)

    def merge(rows):
        put_xs(rows, (img[rows, :].astype(F32) + acc[rows, :]).astype(BF16).astype(F32))

    tiles(merge)
    pack(1, False)
    a2a_start(1)

    a2a_wait(0)
    unpack(0, True)

    def take_cot(rows):
        cotg[rows, :] = get_xs(rows).astype(BF16)

    tiles(take_cot)
    wo_copy.wait()
    for h in range(2):
        datt[:, 512 * h : 512 * h + 512] = dot_nt(
            cotg[...], wo_v[512 * h : 512 * h + 512, :]
        ).astype(BF16)

    tab = table[...]
    tab_hi = tab.astype(BF16)
    rest = tab - tab_hi.astype(F32)
    tab_mid = rest.astype(BF16)
    tab_lo = (rest - tab_mid.astype(F32)).astype(BF16)
    lane = lax.broadcasted_iota(jnp.int32, (256, 128), 1)
    source = lax.broadcasted_iota(jnp.int32, (256, 128), 0)
    for jp in range(8):
        wanted = (lane // 8) * 15 + lax.rem(lane, 8) - jp + 7
        pick = jnp.where(source == wanted, 1.0, 0.0).astype(BF16)
        wtab[pl.ds(jp, 32, stride=8), :] = (
            dot_nn(tab_hi, pick) + dot_nn(tab_mid, pick) + dot_nn(tab_lo, pick)
        )

    wait_halo_sends(0)
    a2a_wait(1)
    unpack(1, True)

    def norm_mid(rows):
        x = get_xs(rows)
        mg[rows, :] = x
        xh, _ = norm_parts(x)
        na[rows, :] = (xh * gain_a[...]).astype(BF16)

    tiles(norm_mid)

    def make_qkv(k, carry):
        wqkv_copy(k).wait()
        qkv[:, pl.ds(pl.multiple_of(k * CH, CH), CH)] = dot_nn(na[...], wqkv_v[k]).astype(BF16)
        return carry

    lax.fori_loop(0, QCH, make_qkv, 0)

    scale = (D // 32) ** -0.5
    lane64 = lax.broadcasted_iota(jnp.int32, (64, 128), 1)
    lane8 = lax.broadcasted_iota(jnp.int32, (8, 128), 1)
    masks = [(lane64 // 32 == h).astype(F32) for h in range(4)]
    masks16 = [m.astype(BF16) for m in masks]
    zero = jnp.zeros((64, 128), BF16)

    def attend(quad, carry):
        for hp in range(2):
            wa = wtab[pl.ds(pl.multiple_of((4 * quad + 2 * hp) * 8, 8), 8), :]
            wb = wtab[pl.ds(pl.multiple_of((4 * quad + 2 * hp) * 8 + 8, 8), 8), :]
            for ip in range(8):
                s = (7 - ip) * 8
                first = pltpu.roll(wa, (128 - s) % 128, 1)
                second = pltpu.roll(wb, (192 - s) % 128, 1)
                btile[8 * ip : 8 * ip + 8, 128 * hp : 128 * hp + 128] = jnp.where(
                    lane8 < 64, first, second
                )
        at = pl.multiple_of(quad * 128, 128)
        for t in range(4):
            rows = slice(64 * t, 64 * t + 64)
            q = qkv[rows, pl.ds(at, 128)]
            kk = qkv[rows, pl.ds(D + at, 128)]
            vv = qkv[rows, pl.ds(2 * D + at, 128)]
            do = datt[rows, pl.ds(at, 128)]
            qm = jnp.concatenate([q * m for m in masks16], axis=0)
            dom = jnp.concatenate([do * m for m in masks16], axis=0)
            sc = dot_nt(kk, qm) * scale + btile[...]
            p = jnp.exp(sc - jnp.max(sc, axis=0, keepdims=True))
            p = p * (1.0 / jnp.sum(p, axis=0, keepdims=True))
            dp = dot_nt(vv, dom)
            ds = p * (dp - jnp.sum(p * dp, axis=0, keepdims=True)) * scale
            both = jnp.concatenate([p, ds], axis=0)
            both16 = both.astype(BF16)
            pb = both16[:64]
            dsb = both16[64:]
            dv = dot_nn(pb, dom)
            dk = dot_nn(dsb, qm)
            turned = both.T.astype(BF16)
            rhs = jnp.concatenate(
                [jnp.concatenate([vv, zero], axis=1), jnp.concatenate([zero, kk], axis=1)], axis=0
            )
            big = dot_nn(turned, rhs)
            o = sum(big[64 * h : 64 * h + 64, :128] * masks[h] for h in range(4))
            dq = sum(big[64 * h : 64 * h + 64, 128:] * masks[h] for h in range(4))
            att[rows, pl.ds(at, 128)] = o.astype(BF16)
            dqkv[rows, pl.ds(at, 128)] = dq.astype(BF16)
            dqkv[rows, pl.ds(D + at, 128)] = dk.astype(BF16)
            dqkv[rows, pl.ds(2 * D + at, 128)] = dv.astype(BF16)
        return carry

    lax.fori_loop(0, 8, attend, 0)

    for h in range(2):
        cols = slice(512 * h, 512 * h + 512)
        acc[:, cols] = mg[:, cols] + dot_nn(att[...], wo_v[:, cols])
    tiles(lambda rows: put_xs(rows, acc[rows, :]))
    pack(2, True)
    a2a_start(2)

    acc[...] = jnp.zeros((T, D), F32)

    def back_qkv(k, carry):
        acc[...] += dot_nt(dqkv[:, pl.ds(pl.multiple_of(k * CH, CH), CH)], wqkv_v[k])
        return carry

    lax.fori_loop(0, QCH, back_qkv, 0)

    def norm_mid_back(rows):
        dy = acc[rows, :].astype(BF16).astype(F32)
        dx = norm_back(mg[rows, :], dy, gain_a[...]).astype(BF16).astype(F32)
        put_xs(rows, cotg[rows, :].astype(F32) + dx)

    tiles(norm_mid_back)
    pack(3, True)
    a2a_start(3)
    a2a_wait(3)
    unpack(3, False)

    def take_dm(rows):
        x = get_xs(rows)
        mg[rows, :] = x
        na[rows, :] = x.astype(BF16)

    tiles(take_dm)

    def back_project(k, carry):
        before[...] = dot_nt(na[...], wp_v[k])

        def slope_tile(rows):
            put_wid(k, rows, before[rows, :] * s2[k, rows, :].astype(F32))

        tiles(slope_tile)
        send_halos(1, k)
        return carry

    lax.fori_loop(0, NCH, back_project, 0)

    acc[...] = jnp.zeros((T, D), F32)

    def back_expand(k, carry):
        wait_halos(1, k)
        for j in range(CH // 128):
            lanes = slice(128 * j, 128 * j + 128)

            def done(r, v):
                slope = s1[k, 16 * r : 16 * r + 16, lanes].astype(F32)
                act[16 * r : 16 * r + 16, lanes] = (v * slope).astype(BF16)

            conv(k, j, True, done)
        acc[...] += dot_nt(act[...], we_v[k])
        return carry

    lax.fori_loop(0, NCH, back_expand, 0)

    a2a_wait(2)
    unpack(2, False)

    def finish(rows):
        out[rows, :] = get_xs(rows).astype(BF16)
        dy = acc[rows, :].astype(BF16).astype(F32)
        dx = norm_back(img[rows, :].astype(F32), dy, gain_c[...]).astype(BF16).astype(F32)
        dimg[rows, :] = (mg[rows, :] + dx).astype(BF16)

    tiles(finish)
    wait_halo_sends(1)
    for n in range(4):
        a2a_wait_send(n)


def local(
    image, gain_conv, w_expand, kernel_taps, w_project, gain_attn, w_qkv, bias_table, w_out, cotangent
):
    height, breadth, width = image.shape
    vmem = pl.BlockSpec(memory_space=pltpu.VMEM)
    hbm = pl.BlockSpec(memory_space=pl.ANY)
    dma = pltpu.SemaphoreType.DMA
    table = jnp.pad(bias_table.reshape(32, 225), ((0, 0), (0, 31)))
    npeer = 64
    out, dimg = pl.pallas_call(
        kernel,
        out_shape=(
            jax.ShapeDtypeStruct((T, D), BF16),
            jax.ShapeDtypeStruct((T, D), BF16),
        ),
        in_specs=[vmem, vmem, hbm, vmem, hbm, vmem, hbm, vmem, hbm, vmem],
        out_specs=(vmem, vmem),
        scratch_shapes=[
            pltpu.VMEM((NCH, D, CH), BF16),
            pltpu.VMEM((NCH, CH, D), BF16),
            pltpu.VMEM((QCH, D, CH), BF16),
            pltpu.VMEM((D, D), BF16),
            pltpu.VMEM((NCH * CH // 128, T, 128), F32),
            pltpu.VMEM((NCH, T, CH), BF16),
            pltpu.VMEM((NCH, T, CH), BF16),
            pltpu.VMEM((NCH, 4, 16, CH), BF16),
            pltpu.VMEM((2, NCH, 4, 16, CH), BF16),
            pltpu.VMEM((4, 32, 128), F32),
            pltpu.VMEM((2, 4, 16, 128), BF16),
            pltpu.VMEM((2, 2, 4, 16, 128), BF16),
            pltpu.VMEM((4, 16, CH), F32),
            pltpu.VMEM((4, 32, 128), F32),
            pltpu.VMEM((T, CH), F32),
            pltpu.VMEM((T, CH), BF16),
            pltpu.VMEM((T, D), F32),
            pltpu.VMEM((8, T, 128), F32),
            pltpu.VMEM((8 * T, 128), F32),
            pltpu.VMEM((T, D), BF16),
            pltpu.VMEM((4, npeer, 32, 128), BF16),
            pltpu.VMEM((4, npeer, 32, 128), BF16),
            pltpu.VMEM((T, D), BF16),
            pltpu.VMEM((T, D), F32),
            pltpu.VMEM((T, 3 * D), BF16),
            pltpu.VMEM((T, D), BF16),
            pltpu.VMEM((T, D), BF16),
            pltpu.VMEM((T, 3 * D), BF16),
            pltpu.VMEM((256, 128), F32),
            pltpu.VMEM((64, 256), F32),
            dma((4, NCH)),
            dma((2, NCH, 4)),
            dma((2, NCH, 4)),
            dma((2, 2, 4)),
            dma((2, 2, 4)),
            dma((4,)),
            dma((4,)),
            dma((4,)),
        ],
        compiler_params=pltpu.CompilerParams(
            collective_id=0, has_side_effects=True, vmem_limit_bytes=62 * 1024 * 1024
        ),
        cost_estimate=pl.CostEstimate(
            flops=13_000_000_000, bytes_accessed=27_000_000, transcendentals=5_000_000
        ),
    )(
        image.reshape(T, D),
        gain_conv.reshape(1, D),
        w_expand,
        kernel_taps,
        w_project,
        gain_attn.reshape(1, D),
        w_qkv,
        table,
        w_out,
        cotangent.reshape(T, D),
    )
    return out.reshape(height, breadth, width), dimg.reshape(height, breadth, width)


def solution(mesh):
    whole = P("rows", "cols", None)
    return jax.shard_map(
        local,
        mesh=mesh,
        in_specs=(whole, P(), P(), P(), P(), P(), P(), P(), P(), whole),
        out_specs=(whole, whole),
        check_vma=False,
    )
```

```python
import jax
import jax.numpy as jnp
from jax import lax
from jax.experimental import pallas as pl
from jax.experimental.pallas import tpu as pltpu
from jax.sharding import PartitionSpec as P

F32 = jnp.float32
BF16 = jnp.bfloat16
MESH = pl.DeviceIdType.MESH
EPS = 1e-05
GRID = 8
T = 256
D = 1024
E = 4096
CH = 1024
NCH = E // CH
LT = CH // 128
QCH = 3 * D // CH
NT = (((1,), (1,)), ((), ()))


def dot_nt(a, b):
    return lax.dot_general(a, b, NT, preferred_element_type=F32)


def dot_nn(a, b):
    return jnp.dot(a, b, preferred_element_type=F32)


def gelu_parts(v):
    e = jnp.exp2(v * v * (-0.5 * 1.4426950408889634))
    u = 1.0 + jnp.abs(v) * (0.3275911 * 0.7071067811865476)
    t = pl.reciprocal(u, approx=True)
    t = t * (2.0 - u * t)
    poly = t * (0.5 * 1.061405429) + (0.5 * -1.453152027)
    poly = poly * t + (0.5 * 1.421413741)
    poly = poly * t + (0.5 * -0.284496736)
    poly = poly * t + (0.5 * 0.254829592)
    tail = poly * t * e
    cdf = jnp.where(v >= 0, 1.0 - tail, tail)
    return cdf, e * 0.3989422804014327


def norm_parts(x):
    c = x - jnp.mean(x, axis=-1, keepdims=True)
    r = lax.rsqrt(jnp.mean(c * c, axis=-1, keepdims=True) + EPS)
    return c * r, r

def norm_back(x, dy, gain):
    xh, r = norm_parts(x)
    dg = dy * gain
    m1 = jnp.mean(dg, axis=-1, keepdims=True)
    m2 = jnp.mean(dg * xh, axis=-1, keepdims=True)
    return (dg - m1 - xh * m2) * r


def kernel(
    img,
    gain_c,
    we,
    kern,
    wp,
    gain_a,
    wqkv,
    table,
    wo,
    cot,
    out,
    d_normed,
    d_mid,
    we_v,
    wp_v,
    wqkv_v,
    wo_v,
    wid,
    s1,
    s2,
    hs,
    hr,
    cs,
    csb,
    cr,
    hrf,
    crf,
    before_a,
    before_b,
    act_a,
    act_b,
    acc,
    xs,
    ys,
    na,
    send,
    recv,
    cotg,
    mg,
    qkv,
    datt,
    att,
    dqkv,
    tpad,
    wtab,
    btile,
    w_sem,
    hsend_sem,
    hrecv_sem,
    csend_sem,
    crecv_sem,
    asend_sem,
    arecv_sem,
    aown_sem,
):
    nrow = lax.axis_size("rows")
    ncol = lax.axis_size("cols")
    R = lax.axis_index("rows")
    C = lax.axis_index("cols")
    core = lax.rem(R, 2)
    me = (R // 2) * ncol + C
    npeer = (nrow // 2) * ncol

    def we_copy(k):
        return pltpu.make_async_copy(
            we.at[:, pl.ds(pl.multiple_of(k * CH, CH), CH)], we_v.at[k], w_sem.at[0, k]
        )

    def wp_copy(k):
        return pltpu.make_async_copy(
            wp.at[pl.ds(pl.multiple_of(k * CH, CH), CH), :], wp_v.at[k], w_sem.at[1, k]
        )

    def wqkv_copy(k):
        return pltpu.make_async_copy(
            wqkv.at[:, pl.ds(pl.multiple_of(k * CH, CH), CH)], wqkv_v.at[k], w_sem.at[2, k]
        )

    wo_copy = pltpu.make_async_copy(wo, wo_v, w_sem.at[3, 0])
    for k in range(NCH):
        we_copy(k).start()
    wo_copy.start()
    for k in range(NCH):
        wp_copy(k).start()
    for k in range(QCH):
        wqkv_copy(k).start()

    barrier = pltpu.get_barrier_semaphore()

    def peer_coord(d):
        return (2 * (d // ncol) + core, lax.rem(d, ncol))

    def greet(q, carry):
        pr, pc = peer_coord(lax.rem(me + q, npeer))
        pl.semaphore_signal(barrier, inc=1, device_id=(pr, pc), device_id_type=MESH)
        return carry

    lax.fori_loop(1, npeer, greet, 0)
    has_u = R > 0
    has_d = R < nrow - 1
    has_l = C > 0
    has_r = C < ncol - 1
    for dr, cond_r in ((-1, has_u), (1, has_d)):
        for dc, cond_c in ((-1, has_l), (0, None), (1, has_r)):
            cond = cond_r if cond_c is None else jnp.logical_and(cond_r, cond_c)

            @pl.when(cond)
            def _():
                pl.semaphore_signal(
                    barrier, inc=1, device_id=(R + dr, C + dc), device_id_type=MESH
                )

    sides = ((-1, 0, has_u), (1, 0, has_d), (0, -1, has_l), (0, 1, has_r))
    corners = (
        (-1, -1, jnp.logical_and(has_u, has_l)),
        (-1, 1, jnp.logical_and(has_u, has_r)),
        (1, -1, jnp.logical_and(has_d, has_l)),
        (1, 1, jnp.logical_and(has_d, has_r)),
    )
    for s, (_, _, cond) in enumerate(sides):

        @pl.when(jnp.logical_not(cond))
        def _():
            for way in range(2):
                hr[way, :, s] = jnp.zeros((NCH, 16, CH), BF16)

    for s, (_, _, cond) in enumerate(corners):

        @pl.when(jnp.logical_not(cond))
        def _():
            for way in range(2):
                cr[way, :, s] = jnp.zeros((2, 16, 128), BF16)

    def side_copy(way, k, s):
        dr, dc, _ = sides[s]
        return pltpu.make_async_remote_copy(
            src_ref=hs.at[k, s],
            dst_ref=hr.at[way, k, s ^ 1],
            send_sem=hsend_sem.at[way, k, s],
            recv_sem=hrecv_sem.at[way, k, s ^ 1],
            device_id=(R + dr, C + dc),
            device_id_type=MESH,
        )

    def side_recv(way, k, s):
        return pltpu.make_async_copy(hs.at[k, s], hr.at[way, k, s], hrecv_sem.at[way, k, s])

    def corner_copy(way, half, s):
        dr, dc, _ = corners[s]
        return pltpu.make_async_remote_copy(
            src_ref=csb.at[half, s],
            dst_ref=cr.at[way, half, 3 - s],
            send_sem=csend_sem.at[way, half, s],
            recv_sem=crecv_sem.at[way, half, 3 - s],
            device_id=(R + dr, C + dc),
            device_id_type=MESH,
        )

    def corner_recv(way, half, s):
        return pltpu.make_async_copy(
            csb.at[half, s], cr.at[way, half, s], crecv_sem.at[way, half, s]
        )

    def send_halos(way, k):
        for j in range(LT):
            lanes = slice(128 * j, 128 * j + 128)
            tile = LT * k + j
            hs[k, 0, :, lanes] = wid[tile, 0:16, :].astype(BF16)
            hs[k, 1, :, lanes] = wid[tile, T - 16 : T, :].astype(BF16)
            hs[k, 2, :, lanes] = wid[tile, pl.ds(0, 16, stride=16), :].astype(BF16)
            hs[k, 3, :, lanes] = wid[tile, pl.ds(15, 16, stride=16), :].astype(BF16)
            for s, row in enumerate((0, 15, T - 16, T - 1)):
                cs[s, tile : tile + 1, :] = wid[tile, row : row + 1, :]
        for s, (_, _, cond) in enumerate(sides):

            @pl.when(cond)
            def _():
                side_copy(way, k, s).start()

        if k % 2 == 1:
            half = k // 2
            for s, (_, _, cond) in enumerate(corners):
                csb[half, s] = cs[s, 16 * half : 16 * half + 16, :].astype(BF16)

                @pl.when(cond)
                def _():
                    corner_copy(way, half, s).start()

    def wait_halos(way, k):
        for s, (_, _, cond) in enumerate(sides):

            @pl.when(cond)
            def _():
                side_recv(way, k, s).wait()

        if k % 2 == 0:
            half = k // 2
            for s, (_, _, cond) in enumerate(corners):

                @pl.when(cond)
                def _():
                    corner_recv(way, half, s).wait()

                crf[s, 16 * half : 16 * half + 16, :] = cr[way, half, s].astype(F32)

        for s in range(4):
            hrf[s] = hr[way, k, s].astype(F32)

    def wait_halo_sends(way):
        def one(k, carry):
            for s, (_, _, cond) in enumerate(sides):

                @pl.when(cond)
                def _():
                    side_copy(way, k, s).wait_send()

            return carry

        lax.fori_loop(0, NCH, one, 0)
        for half in range(2):
            for s, (_, _, cond) in enumerate(corners):

                @pl.when(cond)
                def _():
                    corner_copy(way, half, s).wait_send()

    def a2a_start(n):
        def one(q, carry):
            d = lax.rem(me + q, npeer)
            pltpu.make_async_remote_copy(
                src_ref=send.at[n, d],
                dst_ref=recv.at[n, me],
                send_sem=asend_sem.at[n],
                recv_sem=arecv_sem.at[n],
                device_id=peer_coord(d),
                device_id_type=MESH,
            ).start()
            return carry

        lax.fori_loop(1, npeer, one, 0)
        pltpu.make_async_copy(send.at[n, me], recv.at[n, me], aown_sem.at[n]).start()

    def a2a_wait(n):
        part = pl.ds(0, npeer - 1)
        pltpu.make_async_copy(send.at[n, me], recv.at[n, me], aown_sem.at[n]).wait()
        pltpu.make_async_copy(send.at[n, part], recv.at[n, part], arecv_sem.at[n]).wait()

    def a2a_wait_send(n):
        part = pl.ds(0, npeer - 1)
        pltpu.make_async_copy(send.at[n, part], recv.at[n, part], asend_sem.at[n]).wait()

    def pack(n, grouped):
        for b in range(8):
            for t in range(4):
                rows = pl.ds(64 * t, 64) if grouped else pl.ds(t, 64, stride=4)
                ys[pl.ds(4 * b + t, 64, stride=32), :] = xs[b, rows, :]
        send[n] = ys[...].reshape(64, 32, 128).astype(BF16)

    def unpack(n, grouped):
        ys[...] = recv[n].astype(F32).reshape(2048, 128)
        for b in range(8):
            for t in range(4):
                rows = pl.ds(64 * t, 64) if grouped else pl.ds(t, 64, stride=4)
                xs[b, rows, :] = ys[pl.ds(4 * b + t, 64, stride=32), :]

    def put_xs(rows, value):
        for b in range(8):
            xs[b, rows, :] = value[:, 128 * b : 128 * b + 128]

    def get_xs(rows):
        return jnp.concatenate([xs[b, rows, :] for b in range(8)], axis=1)

    def put_wid(k, rows, value):
        for j in range(LT):
            wid[LT * k + j, rows, :] = value[:, 128 * j : 128 * j + 128]

    def tiles(body, size=32):
        def one(i, carry):
            body(pl.ds(pl.multiple_of(i * size, size), size))
            return carry

        lax.fori_loop(0, T // size, one, 0)

    def norm_in(rows):
        xh, _ = norm_parts(img[rows, :].astype(F32))
        na[rows, :] = (xh * gain_c[...]).astype(BF16)
        put_xs(rows, cot[rows, :].astype(F32))

    tiles(norm_in)
    pack(0, False)

    n_other = (has_u.astype(jnp.int32) + has_d.astype(jnp.int32)) * (
        1 + has_l.astype(jnp.int32) + has_r.astype(jnp.int32)
    )
    befores = (before_a, before_b)
    acts = (act_a, act_b)

    def widen(k):
        for i in range(T // 16):
            rows = slice(16 * i, 16 * i + 16)
            v = befores[k % 2][rows, :]
            cdf, pdf = gelu_parts(v)
            put_wid(k, rows, v * cdf)
            s1[k, rows, :] = (cdf + v * pdf).astype(BF16)

    for k in range(NCH + 1):
        if k < NCH:
            we_copy(k).wait()
            befores[k % 2][...] = dot_nn(na[...], we_v[k])
        if k >= 1:
            widen(k - 1)
            if k == 1:
                pl.semaphore_wait(barrier, npeer - 1 + n_other)
            send_halos(0, k - 1)
            if k == 2:
                a2a_start(0)

    iota16 = lax.broadcasted_iota(jnp.int32, (16, 128), 0)
    at_first = iota16 == 0
    at_last = iota16 == 15

    def conv(k, j, flip, done):
        lanes = slice(128 * j, 128 * j + 128)
        wide = slice(k * CH + 128 * j, k * CH + 128 * j + 128)
        w = [
            [kern[2 - a if flip else a, pl.ds(2 - b if flip else b, 1), wide] for b in range(3)]
            for a in range(3)
        ]
        sums = {}
        for r in range(-1, 17):
            if r == -1 or r == 16:
                low = r == 16
                x = hrf[1 if low else 0, :, lanes]
                cell = slice(LT * k + j, LT * k + j + 1)
                left = crf[2 if low else 0, cell, :]
                right = crf[3 if low else 1, cell, :]
            else:
                x = wid[LT * k + j, 16 * r : 16 * r + 16, :]
                left = hrf[2, r : r + 1, lanes]
                right = hrf[3, r : r + 1, lanes]
            xl = jnp.where(at_first, left, pltpu.roll(x, 1, 0))
            xr = jnp.where(at_last, right, pltpu.roll(x, 15, 0))
            for a in range(3):
                ro = r - a + 1
                if 0 <= ro < 16:
                    part = xl * w[a][0] + x * w[a][1] + xr * w[a][2]
                    sums[ro] = sums[ro] + part if ro in sums else part
            if r >= 1:
                done(r - 1, sums.pop(r - 1))

    for k in range(NCH + 1):
        if k >= 1:
            wp_copy(k - 1).wait()
        if k < NCH:
            wait_halos(0, k)
            for j in range(LT):
                lanes = slice(128 * j, 128 * j + 128)

                def done(r, v):
                    cdf, pdf = gelu_parts(v)
                    acts[k % 2][16 * r : 16 * r + 16, lanes] = (v * cdf).astype(BF16)
                    s2[k, 16 * r : 16 * r + 16, lanes] = (cdf + v * pdf).astype(BF16)

                conv(k, j, False, done)
        if k >= 1:
            part = dot_nn(acts[(k - 1) % 2][...], wp_v[k - 1])
            acc[...] = part if k == 1 else acc[...] + part

    def merge(rows):
        put_xs(rows, (img[rows, :].astype(F32) + acc[rows, :]).astype(BF16).astype(F32))

    tiles(merge)
    pack(1, False)
    a2a_start(1)

    a2a_wait(0)
    unpack(0, True)

    def take_cot(rows):
        cotg[rows, :] = get_xs(rows).astype(BF16)

    tiles(take_cot)
    wo_copy.wait()
    for h in range(2):
        datt[:, 512 * h : 512 * h + 512] = dot_nt(
            cotg[...], wo_v[512 * h : 512 * h + 512, :]
        ).astype(BF16)

    tpad[...] = jnp.zeros((32, 128), F32)
    halves = [None, None]
    for di in range(15):
        tpad[:, 0:15] = table[:, di, :]
        moved = tpad[...]
        if di % 8:
            moved = pltpu.roll(moved, 16 * (di % 8), 1)
        old = halves[di // 8]
        halves[di // 8] = moved if old is None else old + moved
    tab = jnp.concatenate(halves, axis=1)
    tab_hi = tab.astype(BF16)
    rest = tab - tab_hi.astype(F32)
    tab_mid = rest.astype(BF16)
    tab_lo = (rest - tab_mid.astype(F32)).astype(BF16)
    lane = lax.broadcasted_iota(jnp.int32, (256, 128), 1)
    source = lax.broadcasted_iota(jnp.int32, (256, 128), 0)
    for jp in range(8):
        wanted = (lane // 8) * 16 + lax.rem(lane, 8) - jp + 7
        pick = jnp.where(source == wanted, 1.0, 0.0).astype(BF16)
        wtab[pl.ds(jp, 32, stride=8), :] = (
            dot_nn(tab_hi, pick) + dot_nn(tab_mid, pick) + dot_nn(tab_lo, pick)
        )

    wait_halo_sends(0)
    a2a_wait(1)
    unpack(1, True)

    def norm_mid(rows):
        x = get_xs(rows)
        mg[rows, :] = x
        xh, _ = norm_parts(x)
        na[rows, :] = (xh * gain_a[...]).astype(BF16)

    tiles(norm_mid)

    def make_qkv(k, carry):
        wqkv_copy(k).wait()
        qkv[:, pl.ds(pl.multiple_of(k * CH, CH), CH)] = dot_nn(na[...], wqkv_v[k]).astype(BF16)
        return carry

    lax.fori_loop(0, QCH, make_qkv, 0)

    scale = (D // 32) ** -0.5
    lane64 = lax.broadcasted_iota(jnp.int32, (64, 128), 1)
    lane8 = lax.broadcasted_iota(jnp.int32, (8, 128), 1)
    masks = [(lane64 // 32 == h).astype(F32) for h in range(4)]
    masks16 = [m.astype(BF16) for m in masks]
    zero = jnp.zeros((64, 128), BF16)

    def attend(quad, carry):
        for hp in range(2):
            wa = wtab[pl.ds(pl.multiple_of((4 * quad + 2 * hp) * 8, 8), 8), :]
            wb = wtab[pl.ds(pl.multiple_of((4 * quad + 2 * hp) * 8 + 8, 8), 8), :]
            for ip in range(8):
                s = (7 - ip) * 8
                first = pltpu.roll(wa, (128 - s) % 128, 1)
                second = pltpu.roll(wb, (192 - s) % 128, 1)
                btile[8 * ip : 8 * ip + 8, 128 * hp : 128 * hp + 128] = jnp.where(
                    lane8 < 64, first, second
                )
        at = pl.multiple_of(quad * 128, 128)
        for t in range(4):
            rows = slice(64 * t, 64 * t + 64)
            q = qkv[rows, pl.ds(at, 128)]
            kk = qkv[rows, pl.ds(D + at, 128)]
            vv = qkv[rows, pl.ds(2 * D + at, 128)]
            do = datt[rows, pl.ds(at, 128)]
            qm = jnp.concatenate([q * m for m in masks16], axis=0)
            dom = jnp.concatenate([do * m for m in masks16], axis=0)
            sc = dot_nt(kk, qm) * scale + btile[...]
            p = jnp.exp(sc - jnp.max(sc, axis=0, keepdims=True))
            p = p * (1.0 / jnp.sum(p, axis=0, keepdims=True))
            dp = dot_nt(vv, dom)
            ds = p * (dp - jnp.sum(p * dp, axis=0, keepdims=True)) * scale
            both = jnp.concatenate([p, ds], axis=0)
            both16 = both.astype(BF16)
            pb = both16[:64]
            dsb = both16[64:]
            dv = dot_nn(pb, dom)
            dk = dot_nn(dsb, qm)
            turned = both.T.astype(BF16)
            rhs = jnp.concatenate(
                [jnp.concatenate([vv, zero], axis=1), jnp.concatenate([zero, kk], axis=1)], axis=0
            )
            big = dot_nn(turned, rhs)
            o = sum(big[64 * h : 64 * h + 64, :128] * masks[h] for h in range(4))
            dq = sum(big[64 * h : 64 * h + 64, 128:] * masks[h] for h in range(4))
            att[rows, pl.ds(at, 128)] = o.astype(BF16)
            dqkv[rows, pl.ds(at, 128)] = dq.astype(BF16)
            dqkv[rows, pl.ds(D + at, 128)] = dk.astype(BF16)
            dqkv[rows, pl.ds(2 * D + at, 128)] = dv.astype(BF16)
        return carry

    lax.fori_loop(0, 8, attend, 0)

    for h in range(2):
        cols = slice(512 * h, 512 * h + 512)
        acc[:, cols] = mg[:, cols] + dot_nn(att[...], wo_v[:, cols])
    tiles(lambda rows: put_xs(rows, acc[rows, :]))
    pack(2, True)
    a2a_start(2)

    def back_qkv(k):
        part = dot_nt(dqkv[:, CH * k : CH * k + CH], wqkv_v[k])
        acc[...] = part if k == 0 else acc[...] + part

    for k in range(QCH):
        back_qkv(k)

    def norm_mid_back(rows):
        dy = acc[rows, :].astype(BF16).astype(F32)
        dx = norm_back(mg[rows, :], dy, gain_a[...]).astype(BF16).astype(F32)
        put_xs(rows, cotg[rows, :].astype(F32) + dx)

    tiles(norm_mid_back)
    pack(3, True)
    a2a_start(3)
    a2a_wait(3)
    unpack(3, False)

    def take_dm(rows):
        na[rows, :] = get_xs(rows).astype(BF16)

    tiles(take_dm)

    def slope(k):
        for i in range(T // 16):
            rows = slice(16 * i, 16 * i + 16)
            put_wid(k, rows, befores[k % 2][rows, :] * s2[k, rows, :].astype(F32))

    for k in range(NCH + 1):
        if k < NCH:
            befores[k % 2][...] = dot_nt(na[...], wp_v[k])
        if k >= 1:
            slope(k - 1)
            send_halos(1, k - 1)

    for k in range(NCH + 1):
        if k < NCH:
            wait_halos(1, k)
            for j in range(LT):
                lanes = slice(128 * j, 128 * j + 128)

                def done(r, v):
                    back = s1[k, 16 * r : 16 * r + 16, lanes].astype(F32)
                    acts[k % 2][16 * r : 16 * r + 16, lanes] = (v * back).astype(BF16)

                conv(k, j, True, done)
        if k >= 1:
            part = dot_nt(acts[(k - 1) % 2][...], we_v[k - 1])
            acc[...] = part if k == 1 else acc[...] + part

    a2a_wait(2)
    unpack(2, False)

    def finish(rows):
        out[rows, :] = get_xs(rows).astype(BF16)
        d_normed[rows, :] = acc[rows, :].astype(BF16)
        d_mid[rows, :] = na[rows, :]

    tiles(finish)
    wait_halo_sends(1)
    for n in range(4):
        a2a_wait_send(n)


def last_kernel(img, gain_c, sent, d_normed, d_mid, out, dimg):
    out[...] = sent[...]
    dy = d_normed[...].astype(F32)
    dx = norm_back(img[...].astype(F32), dy, gain_c[...]).astype(BF16).astype(F32)
    dimg[...] = (d_mid[...].astype(F32) + dx).astype(BF16)


def local(
    image, gain_conv, w_expand, kernel_taps, w_project, gain_attn, w_qkv, bias_table, w_out, cotangent
):
    height, breadth, width = image.shape
    vmem = pl.BlockSpec(memory_space=pltpu.VMEM)
    hbm = pl.BlockSpec(memory_space=pl.ANY)
    dma = pltpu.SemaphoreType.DMA
    npeer = 64
    image = image.reshape(T, D)
    gain_conv = gain_conv.reshape(1, D)
    whole = jax.ShapeDtypeStruct((T, D), BF16)
    sent, d_normed, d_mid = pl.pallas_call(
        kernel,
        out_shape=(whole, whole, whole),
        in_specs=[vmem, vmem, hbm, vmem, hbm, vmem, hbm, vmem, hbm, vmem],
        out_specs=(vmem, vmem, vmem),
        scratch_shapes=[
            pltpu.VMEM((NCH, D, CH), BF16),
            pltpu.VMEM((NCH, CH, D), BF16),
            pltpu.VMEM((QCH, D, CH), BF16),
            pltpu.VMEM((D, D), BF16),
            pltpu.VMEM((NCH * CH // 128, T, 128), F32),
            pltpu.VMEM((NCH, T, CH), BF16),
            pltpu.VMEM((NCH, T, CH), BF16),
            pltpu.VMEM((NCH, 4, 16, CH), BF16),
            pltpu.VMEM((2, NCH, 4, 16, CH), BF16),
            pltpu.VMEM((4, 32, 128), F32),
            pltpu.VMEM((2, 4, 16, 128), BF16),
            pltpu.VMEM((2, 2, 4, 16, 128), BF16),
            pltpu.VMEM((4, 16, CH), F32),
            pltpu.VMEM((4, 32, 128), F32),
            pltpu.VMEM((T, CH), F32),
            pltpu.VMEM((T, CH), F32),
            pltpu.VMEM((T, CH), BF16),
            pltpu.VMEM((T, CH), BF16),
            pltpu.VMEM((T, D), F32),
            pltpu.VMEM((8, T, 128), F32),
            pltpu.VMEM((8 * T, 128), F32),
            pltpu.VMEM((T, D), BF16),
            pltpu.VMEM((4, npeer, 32, 128), BF16),
            pltpu.VMEM((4, npeer, 32, 128), BF16),
            pltpu.VMEM((T, D), BF16),
            pltpu.VMEM((T, D), F32),
            pltpu.VMEM((T, 3 * D), BF16),
            pltpu.VMEM((T, D), BF16),
            pltpu.VMEM((T, D), BF16),
            pltpu.VMEM((T, 3 * D), BF16),
            pltpu.VMEM((32, 128), F32),
            pltpu.VMEM((256, 128), F32),
            pltpu.VMEM((64, 256), F32),
            dma((4, NCH)),
            dma((2, NCH, 4)),
            dma((2, NCH, 4)),
            dma((2, 2, 4)),
            dma((2, 2, 4)),
            dma((4,)),
            dma((4,)),
            dma((4,)),
        ],
        compiler_params=pltpu.CompilerParams(
            collective_id=0, has_side_effects=True, vmem_limit_bytes=62 * 1024 * 1024
        ),
        cost_estimate=pl.CostEstimate(
            flops=13_000_000_000, bytes_accessed=27_000_000, transcendentals=5_000_000
        ),
    )(
        image,
        gain_conv,
        w_expand,
        kernel_taps,
        w_project,
        gain_attn.reshape(1, D),
        w_qkv,
        bias_table,
        w_out,
        cotangent.reshape(T, D),
    )
    rows = pl.BlockSpec((64, D), lambda i: (i, 0))
    out, dimg = pl.pallas_call(
        last_kernel,
        grid=(T // 64,),
        out_shape=(whole, whole),
        in_specs=[rows, pl.BlockSpec((1, D), lambda i: (0, 0)), rows, rows, rows],
        out_specs=(rows, rows),
    )(image, gain_conv, sent, d_normed, d_mid)
    return out.reshape(height, breadth, width), dimg.reshape(height, breadth, width)


def solution(mesh):
    whole = P("rows", "cols", None)
    return jax.shard_map(
        local,
        mesh=mesh,
        in_specs=(whole, P(), P(), P(), P(), P(), P(), P(), P(), whole),
        out_specs=(whole, whole),
        check_vma=False,
    )
```

```python
import jax
import jax.numpy as jnp
from jax import lax
from jax.experimental import pallas as pl
from jax.experimental.pallas import tpu as pltpu
from jax.sharding import PartitionSpec as P

F32 = jnp.float32
BF16 = jnp.bfloat16
MESH = pl.DeviceIdType.MESH
EPS = 1e-05
GRID = 8
T = 256
D = 1024
E = 4096
CH = 1024
NCH = E // CH
LT = CH // 128
QCH = 3 * D // CH
NT = (((1,), (1,)), ((), ()))


def dot_nt(a, b):
    return lax.dot_general(a, b, NT, preferred_element_type=F32)


def dot_nn(a, b):
    return jnp.dot(a, b, preferred_element_type=F32)


def gelu_parts(v):
    e = jnp.exp2(v * v * (-0.5 * 1.4426950408889634))
    u = 1.0 + jnp.abs(v) * (0.3275911 * 0.7071067811865476)
    t = pl.reciprocal(u, approx=True)
    t = t * (2.0 - u * t)
    poly = t * (0.5 * 1.061405429) + (0.5 * -1.453152027)
    poly = poly * t + (0.5 * 1.421413741)
    poly = poly * t + (0.5 * -0.284496736)
    poly = poly * t + (0.5 * 0.254829592)
    tail = poly * t * e
    cdf = jnp.where(v >= 0, 1.0 - tail, tail)
    return cdf, e * 0.3989422804014327


def norm_parts(x):
    c = x - jnp.mean(x, axis=-1, keepdims=True)
    r = lax.rsqrt(jnp.mean(c * c, axis=-1, keepdims=True) + EPS)
    return c * r, r

def norm_back(x, dy, gain):
    xh, r = norm_parts(x)
    dg = dy * gain
    m1 = jnp.mean(dg, axis=-1, keepdims=True)
    m2 = jnp.mean(dg * xh, axis=-1, keepdims=True)
    return (dg - m1 - xh * m2) * r


def kernel(
    img,
    gain_c,
    we,
    kern,
    wp,
    gain_a,
    wqkv,
    table,
    wo,
    cot,
    out,
    d_normed,
    d_mid,
    we_v,
    wp_v,
    wqkv_v,
    wo_v,
    wid,
    s1,
    s2,
    hs,
    hr,
    cs,
    csb,
    cr,
    hrf,
    crf,
    before_a,
    before_b,
    act_a,
    act_b,
    acc,
    xs,
    ys,
    na,
    send,
    recv,
    cotg,
    mg,
    qkv,
    datt,
    att,
    dqkv,
    tpad,
    wtab,
    btile,
    w_sem,
    hsend_sem,
    hrecv_sem,
    csend_sem,
    crecv_sem,
    asend_sem,
    arecv_sem,
    aown_sem,
):
    nrow = lax.axis_size("rows")
    ncol = lax.axis_size("cols")
    R = lax.axis_index("rows")
    C = lax.axis_index("cols")
    core = lax.rem(R, 2)
    me = (R // 2) * ncol + C
    npeer = (nrow // 2) * ncol

    def we_copy(k):
        return pltpu.make_async_copy(
            we.at[:, pl.ds(pl.multiple_of(k * CH, CH), CH)], we_v.at[k], w_sem.at[0, k]
        )

    def wp_copy(k):
        return pltpu.make_async_copy(
            wp.at[pl.ds(pl.multiple_of(k * CH, CH), CH), :], wp_v.at[k], w_sem.at[1, k]
        )

    def wqkv_copy(k):
        return pltpu.make_async_copy(
            wqkv.at[:, pl.ds(pl.multiple_of(k * CH, CH), CH)], wqkv_v.at[k], w_sem.at[2, k]
        )

    wo_copy = pltpu.make_async_copy(wo, wo_v, w_sem.at[3, 0])
    for k in range(NCH):
        we_copy(k).start()
    wo_copy.start()
    for k in range(NCH):
        wp_copy(k).start()
    for k in range(QCH):
        wqkv_copy(k).start()

    barrier = pltpu.get_barrier_semaphore()

    def peer_coord(d):
        return (2 * (d // ncol) + core, lax.rem(d, ncol))

    def greet(q, carry):
        pr, pc = peer_coord(lax.rem(me + q, npeer))
        pl.semaphore_signal(barrier, inc=1, device_id=(pr, pc), device_id_type=MESH)
        return carry

    lax.fori_loop(1, npeer, greet, 0)
    has_u = R > 0
    has_d = R < nrow - 1
    has_l = C > 0
    has_r = C < ncol - 1
    for dr, cond_r in ((-1, has_u), (1, has_d)):
        for dc, cond_c in ((-1, has_l), (0, None), (1, has_r)):
            cond = cond_r if cond_c is None else jnp.logical_and(cond_r, cond_c)

            @pl.when(cond)
            def _():
                pl.semaphore_signal(
                    barrier, inc=1, device_id=(R + dr, C + dc), device_id_type=MESH
                )

    sides = ((-1, 0, has_u), (1, 0, has_d), (0, -1, has_l), (0, 1, has_r))
    corners = (
        (-1, -1, jnp.logical_and(has_u, has_l)),
        (-1, 1, jnp.logical_and(has_u, has_r)),
        (1, -1, jnp.logical_and(has_d, has_l)),
        (1, 1, jnp.logical_and(has_d, has_r)),
    )
    for s, (_, _, cond) in enumerate(sides):

        @pl.when(jnp.logical_not(cond))
        def _():
            for way in range(2):
                hr[way, :, s] = jnp.zeros((NCH, 16, CH), BF16)

    for s, (_, _, cond) in enumerate(corners):

        @pl.when(jnp.logical_not(cond))
        def _():
            for way in range(2):
                cr[way, :, s] = jnp.zeros((2, 16, 128), BF16)

    def side_copy(way, k, s):
        dr, dc, _ = sides[s]
        return pltpu.make_async_remote_copy(
            src_ref=hs.at[k, s],
            dst_ref=hr.at[way, k, s ^ 1],
            send_sem=hsend_sem.at[way, k, s],
            recv_sem=hrecv_sem.at[way, k, s ^ 1],
            device_id=(R + dr, C + dc),
            device_id_type=MESH,
        )

    def side_recv(way, k, s):
        return pltpu.make_async_copy(hs.at[k, s], hr.at[way, k, s], hrecv_sem.at[way, k, s])

    def corner_copy(way, half, s):
        dr, dc, _ = corners[s]
        return pltpu.make_async_remote_copy(
            src_ref=csb.at[half, s],
            dst_ref=cr.at[way, half, 3 - s],
            send_sem=csend_sem.at[way, half, s],
            recv_sem=crecv_sem.at[way, half, 3 - s],
            device_id=(R + dr, C + dc),
            device_id_type=MESH,
        )

    def corner_recv(way, half, s):
        return pltpu.make_async_copy(
            csb.at[half, s], cr.at[way, half, s], crecv_sem.at[way, half, s]
        )

    def send_halos(way, k):
        for j in range(LT):
            lanes = slice(128 * j, 128 * j + 128)
            tile = LT * k + j
            hs[k, 0, :, lanes] = wid[tile, 0:16, :].astype(BF16)
            hs[k, 1, :, lanes] = wid[tile, T - 16 : T, :].astype(BF16)
            hs[k, 2, :, lanes] = wid[tile, pl.ds(0, 16, stride=16), :].astype(BF16)
            hs[k, 3, :, lanes] = wid[tile, pl.ds(15, 16, stride=16), :].astype(BF16)
            for s, row in enumerate((0, 15, T - 16, T - 1)):
                cs[s, tile : tile + 1, :] = wid[tile, row : row + 1, :]
        for s, (_, _, cond) in enumerate(sides):

            @pl.when(cond)
            def _():
                side_copy(way, k, s).start()

        if k % 2 == 1:
            half = k // 2
            for s, (_, _, cond) in enumerate(corners):
                csb[half, s] = cs[s, 16 * half : 16 * half + 16, :].astype(BF16)

                @pl.when(cond)
                def _():
                    corner_copy(way, half, s).start()

    def wait_halos(way, k):
        for s, (_, _, cond) in enumerate(sides):

            @pl.when(cond)
            def _():
                side_recv(way, k, s).wait()

        if k % 2 == 0:
            half = k // 2
            for s, (_, _, cond) in enumerate(corners):

                @pl.when(cond)
                def _():
                    corner_recv(way, half, s).wait()

                crf[s, 16 * half : 16 * half + 16, :] = cr[way, half, s].astype(F32)

        for s in range(4):
            hrf[s] = hr[way, k, s].astype(F32)

    def wait_halo_sends(way):
        def one(k, carry):
            for s, (_, _, cond) in enumerate(sides):

                @pl.when(cond)
                def _():
                    side_copy(way, k, s).wait_send()

            return carry

        lax.fori_loop(0, NCH, one, 0)
        for half in range(2):
            for s, (_, _, cond) in enumerate(corners):

                @pl.when(cond)
                def _():
                    corner_copy(way, half, s).wait_send()

    def a2a_start(n):
        def one(q, carry):
            d = lax.rem(me + q, npeer)
            pltpu.make_async_remote_copy(
                src_ref=send.at[n, d],
                dst_ref=recv.at[n, me],
                send_sem=asend_sem.at[n],
                recv_sem=arecv_sem.at[n],
                device_id=peer_coord(d),
                device_id_type=MESH,
            ).start()
            return carry

        lax.fori_loop(1, npeer, one, 0)
        pltpu.make_async_copy(send.at[n, me], recv.at[n, me], aown_sem.at[n]).start()

    def a2a_wait(n):
        part = pl.ds(0, npeer - 1)
        pltpu.make_async_copy(send.at[n, me], recv.at[n, me], aown_sem.at[n]).wait()
        pltpu.make_async_copy(send.at[n, part], recv.at[n, part], arecv_sem.at[n]).wait()

    def a2a_wait_send(n):
        part = pl.ds(0, npeer - 1)
        pltpu.make_async_copy(send.at[n, part], recv.at[n, part], asend_sem.at[n]).wait()

    def pack(n, grouped):
        def gather(b, carry):
            for t in range(4):
                rows = pl.ds(64 * t, 64) if grouped else pl.ds(t, 64, stride=4)
                ys[pl.ds(4 * b + t, 64, stride=32), :] = xs[b, rows, :]
            return carry

        lax.fori_loop(0, 8, gather, 0)

        def narrow(d, carry):
            block = ys[pl.ds(pl.multiple_of(d * 256, 256), 256), :]
            send[n, pl.ds(d * 8, 8)] = block.reshape(8, 32, 128).astype(BF16)
            return carry

        lax.fori_loop(0, 8, narrow, 0)

    def unpack(n, grouped):
        def widen_rows(d, carry):
            block = recv[n, pl.ds(d * 8, 8)].astype(F32).reshape(256, 128)
            ys[pl.ds(pl.multiple_of(d * 256, 256), 256), :] = block
            return carry

        lax.fori_loop(0, 8, widen_rows, 0)

        def spread(b, carry):
            for t in range(4):
                rows = pl.ds(64 * t, 64) if grouped else pl.ds(t, 64, stride=4)
                xs[b, rows, :] = ys[pl.ds(4 * b + t, 64, stride=32), :]
            return carry

        lax.fori_loop(0, 8, spread, 0)

    def put_xs(rows, value):
        for b in range(8):
            xs[b, rows, :] = value[:, 128 * b : 128 * b + 128]

    def get_xs(rows):
        return jnp.concatenate([xs[b, rows, :] for b in range(8)], axis=1)

    def put_wid(k, rows, value):
        for j in range(LT):
            wid[LT * k + j, rows, :] = value[:, 128 * j : 128 * j + 128]

    def tiles(body, size=32):
        def one(i, carry):
            body(pl.ds(pl.multiple_of(i * size, size), size))
            return carry

        lax.fori_loop(0, T // size, one, 0)

    def norm_in(rows):
        xh, _ = norm_parts(img[rows, :].astype(F32))
        na[rows, :] = (xh * gain_c[...]).astype(BF16)
        put_xs(rows, cot[rows, :].astype(F32))

    tiles(norm_in)
    pack(0, False)

    n_other = (has_u.astype(jnp.int32) + has_d.astype(jnp.int32)) * (
        1 + has_l.astype(jnp.int32) + has_r.astype(jnp.int32)
    )
    befores = (before_a, before_b)
    acts = (act_a, act_b)

    def widen(k):
        for i in range(T // 16):
            rows = slice(16 * i, 16 * i + 16)
            v = befores[k % 2][rows, :]
            cdf, pdf = gelu_parts(v)
            put_wid(k, rows, v * cdf)
            s1[k, rows, :] = (cdf + v * pdf).astype(BF16)

    for k in range(NCH + 1):
        if k < NCH:
            we_copy(k).wait()
            befores[k % 2][...] = dot_nn(na[...], we_v[k])
        if k >= 1:
            widen(k - 1)
            if k == 1:
                pl.semaphore_wait(barrier, npeer - 1 + n_other)
            send_halos(0, k - 1)
    a2a_start(0)

    iota16 = lax.broadcasted_iota(jnp.int32, (16, 128), 0)
    at_first = iota16 == 0
    at_last = iota16 == 15

    def conv(k, j, flip, done):
        lanes = slice(128 * j, 128 * j + 128)
        wide = slice(k * CH + 128 * j, k * CH + 128 * j + 128)
        w = [
            [kern[2 - a if flip else a, pl.ds(2 - b if flip else b, 1), wide] for b in range(3)]
            for a in range(3)
        ]
        sums = {}
        for r in range(-1, 17):
            if r == -1 or r == 16:
                low = r == 16
                x = hrf[1 if low else 0, :, lanes]
                cell = slice(LT * k + j, LT * k + j + 1)
                left = crf[2 if low else 0, cell, :]
                right = crf[3 if low else 1, cell, :]
            else:
                x = wid[LT * k + j, 16 * r : 16 * r + 16, :]
                left = hrf[2, r : r + 1, lanes]
                right = hrf[3, r : r + 1, lanes]
            xl = jnp.where(at_first, left, pltpu.roll(x, 1, 0))
            xr = jnp.where(at_last, right, pltpu.roll(x, 15, 0))
            for a in range(3):
                ro = r - a + 1
                if 0 <= ro < 16:
                    part = xl * w[a][0] + x * w[a][1] + xr * w[a][2]
                    sums[ro] = sums[ro] + part if ro in sums else part
            if r >= 1:
                done(r - 1, sums.pop(r - 1))

    for k in range(NCH + 1):
        if k >= 1:
            wp_copy(k - 1).wait()
        if k < NCH:
            wait_halos(0, k)
            for j in range(LT):
                lanes = slice(128 * j, 128 * j + 128)

                def done(r, v):
                    cdf, pdf = gelu_parts(v)
                    acts[k % 2][16 * r : 16 * r + 16, lanes] = (v * cdf).astype(BF16)
                    s2[k, 16 * r : 16 * r + 16, lanes] = (cdf + v * pdf).astype(BF16)

                conv(k, j, False, done)
        if k >= 1:
            part = dot_nn(acts[(k - 1) % 2][...], wp_v[k - 1])
            acc[...] = part if k == 1 else acc[...] + part

    def merge(rows):
        put_xs(rows, (img[rows, :].astype(F32) + acc[rows, :]).astype(BF16).astype(F32))

    tiles(merge)
    pack(1, False)
    a2a_start(1)

    a2a_wait(0)
    unpack(0, True)

    def take_cot(rows):
        cotg[rows, :] = get_xs(rows).astype(BF16)

    tiles(take_cot)
    wo_copy.wait()
    for h in range(2):
        datt[:, 512 * h : 512 * h + 512] = dot_nt(
            cotg[...], wo_v[512 * h : 512 * h + 512, :]
        ).astype(BF16)

    tpad[...] = jnp.zeros((32, 128), F32)
    halves = [None, None]
    for di in range(15):
        tpad[:, 0:15] = table[:, di, :]
        moved = tpad[...]
        if di % 8:
            moved = pltpu.roll(moved, 16 * (di % 8), 1)
        old = halves[di // 8]
        halves[di // 8] = moved if old is None else old + moved
    tab = jnp.concatenate(halves, axis=1)
    tab_hi = tab.astype(BF16)
    rest = tab - tab_hi.astype(F32)
    tab_mid = rest.astype(BF16)
    tab_lo = (rest - tab_mid.astype(F32)).astype(BF16)
    lane = lax.broadcasted_iota(jnp.int32, (256, 128), 1)
    source = lax.broadcasted_iota(jnp.int32, (256, 128), 0)
    for jp in range(8):
        wanted = (lane // 8) * 16 + lax.rem(lane, 8) - jp + 7
        pick = jnp.where(source == wanted, 1.0, 0.0).astype(BF16)
        wtab[pl.ds(jp, 32, stride=8), :] = (
            dot_nn(tab_hi, pick) + dot_nn(tab_mid, pick) + dot_nn(tab_lo, pick)
        )

    wait_halo_sends(0)
    a2a_wait(1)
    unpack(1, True)

    def norm_mid(rows):
        x = get_xs(rows)
        mg[rows, :] = x
        xh, _ = norm_parts(x)
        na[rows, :] = (xh * gain_a[...]).astype(BF16)

    tiles(norm_mid)

    def make_qkv(k, carry):
        wqkv_copy(k).wait()
        qkv[:, pl.ds(pl.multiple_of(k * CH, CH), CH)] = dot_nn(na[...], wqkv_v[k]).astype(BF16)
        return carry

    lax.fori_loop(0, QCH, make_qkv, 0)

    scale = (D // 32) ** -0.5
    lane64 = lax.broadcasted_iota(jnp.int32, (64, 128), 1)
    lane8 = lax.broadcasted_iota(jnp.int32, (8, 128), 1)
    masks = [(lane64 // 32 == h).astype(F32) for h in range(4)]
    masks16 = [m.astype(BF16) for m in masks]
    zero = jnp.zeros((64, 128), BF16)

    def stack_heads(x):
        return jnp.concatenate([x * m for m in masks16], axis=0)

    def attend(quad, carry):
        for hp in range(2):
            wa = wtab[pl.ds(pl.multiple_of((4 * quad + 2 * hp) * 8, 8), 8), :]
            wb = wtab[pl.ds(pl.multiple_of((4 * quad + 2 * hp) * 8 + 8, 8), 8), :]
            for ip in range(8):
                s = (7 - ip) * 8
                first = pltpu.roll(wa, (128 - s) % 128, 1)
                second = pltpu.roll(wb, (192 - s) % 128, 1)
                btile[8 * ip : 8 * ip + 8, 128 * hp : 128 * hp + 128] = jnp.where(
                    lane8 < 64, first, second
                )
        at = pl.multiple_of(quad * 128, 128)
        rows = [slice(64 * t, 64 * t + 64) for t in range(4)]
        kk = [qkv[r, pl.ds(D + at, 128)] for r in rows]
        vv = [qkv[r, pl.ds(2 * D + at, 128)] for r in rows]
        qm = [stack_heads(qkv[r, pl.ds(at, 128)]) for r in rows]
        dom = [stack_heads(datt[r, pl.ds(at, 128)]) for r in rows]
        score = [dot_nt(kk[t], qm[t]) for t in range(4)]
        dp = [dot_nt(vv[t], dom[t]) for t in range(4)]
        both = []
        for t in range(4):
            sc = score[t] * scale + btile[...]
            p = jnp.exp(sc - jnp.max(sc, axis=0, keepdims=True))
            p = p * (1.0 / jnp.sum(p, axis=0, keepdims=True))
            ds = p * (dp[t] - jnp.sum(p * dp[t], axis=0, keepdims=True)) * scale
            both.append(jnp.concatenate([p, ds], axis=0))
        for t in range(4):
            turned = jnp.concatenate([dom[t], qm[t]], axis=1)
            d_both = dot_nn(both[t].astype(BF16), turned)
            dqkv[rows[t], pl.ds(D + at, 128)] = d_both[64:, 128:].astype(BF16)
            dqkv[rows[t], pl.ds(2 * D + at, 128)] = d_both[:64, :128].astype(BF16)
        turned = [b.T.astype(BF16) for b in both]
        big = []
        for t in range(4):
            upper = jnp.concatenate([vv[t], zero], axis=1)
            lower = jnp.concatenate([zero, kk[t]], axis=1)
            big.append(dot_nn(turned[t], jnp.concatenate([upper, lower], axis=0)))
        for t in range(4):
            parts = [big[t][64 * h : 64 * h + 64] for h in range(4)]
            o = sum(parts[h][:, :128] * masks[h] for h in range(4))
            dq = sum(parts[h][:, 128:] * masks[h] for h in range(4))
            att[rows[t], pl.ds(at, 128)] = o.astype(BF16)
            dqkv[rows[t], pl.ds(at, 128)] = dq.astype(BF16)
        return carry

    lax.fori_loop(0, 8, attend, 0)

    for h in range(2):
        cols = slice(512 * h, 512 * h + 512)
        acc[:, cols] = mg[:, cols] + dot_nn(att[...], wo_v[:, cols])
    tiles(lambda rows: put_xs(rows, acc[rows, :]))
    pack(2, True)
    a2a_start(2)

    def back_qkv(k):
        part = dot_nt(dqkv[:, CH * k : CH * k + CH], wqkv_v[k])
        acc[...] = part if k == 0 else acc[...] + part

    for k in range(QCH):
        back_qkv(k)

    def norm_mid_back(rows):
        dy = acc[rows, :].astype(BF16).astype(F32)
        dx = norm_back(mg[rows, :], dy, gain_a[...]).astype(BF16).astype(F32)
        put_xs(rows, cotg[rows, :].astype(F32) + dx)

    tiles(norm_mid_back)
    pack(3, True)
    a2a_start(3)

    a2a_wait(2)
    unpack(2, False)

    def take_out(rows):
        out[rows, :] = get_xs(rows).astype(BF16)

    tiles(take_out)
    a2a_wait(3)
    unpack(3, False)

    def take_dm(rows):
        na[rows, :] = get_xs(rows).astype(BF16)

    tiles(take_dm)

    def slope(k):
        for i in range(T // 16):
            rows = slice(16 * i, 16 * i + 16)
            put_wid(k, rows, befores[k % 2][rows, :] * s2[k, rows, :].astype(F32))

    for k in range(NCH + 1):
        if k < NCH:
            befores[k % 2][...] = dot_nt(na[...], wp_v[k])
        if k >= 1:
            slope(k - 1)
            send_halos(1, k - 1)

    for k in range(NCH + 1):
        if k < NCH:
            wait_halos(1, k)
            for j in range(LT):
                lanes = slice(128 * j, 128 * j + 128)

                def done(r, v):
                    back = s1[k, 16 * r : 16 * r + 16, lanes].astype(F32)
                    acts[k % 2][16 * r : 16 * r + 16, lanes] = (v * back).astype(BF16)

                conv(k, j, True, done)
        if k >= 1:
            part = dot_nt(acts[(k - 1) % 2][...], we_v[k - 1])
            acc[...] = part if k == 1 else acc[...] + part

    def finish(rows):
        d_normed[rows, :] = acc[rows, :].astype(BF16)
        d_mid[rows, :] = na[rows, :]

    tiles(finish)
    wait_halo_sends(1)
    for n in range(4):
        a2a_wait_send(n)


def last_kernel(img, gain_c, sent, d_normed, d_mid, out, dimg):
    out[...] = sent[...]
    dy = d_normed[...].astype(F32)
    dx = norm_back(img[...].astype(F32), dy, gain_c[...]).astype(BF16).astype(F32)
    dimg[...] = (d_mid[...].astype(F32) + dx).astype(BF16)


def local(
    image, gain_conv, w_expand, kernel_taps, w_project, gain_attn, w_qkv, bias_table, w_out, cotangent
):
    height, breadth, width = image.shape
    vmem = pl.BlockSpec(memory_space=pltpu.VMEM)
    hbm = pl.BlockSpec(memory_space=pl.ANY)
    dma = pltpu.SemaphoreType.DMA
    npeer = 64
    image = image.reshape(T, D)
    gain_conv = gain_conv.reshape(1, D)
    whole = jax.ShapeDtypeStruct((T, D), BF16)
    sent, d_normed, d_mid = pl.pallas_call(
        kernel,
        out_shape=(whole, whole, whole),
        in_specs=[vmem, vmem, hbm, vmem, hbm, vmem, hbm, vmem, hbm, vmem],
        out_specs=(vmem, vmem, vmem),
        scratch_shapes=[
            pltpu.VMEM((NCH, D, CH), BF16),
            pltpu.VMEM((NCH, CH, D), BF16),
            pltpu.VMEM((QCH, D, CH), BF16),
            pltpu.VMEM((D, D), BF16),
            pltpu.VMEM((NCH * CH // 128, T, 128), F32),
            pltpu.VMEM((NCH, T, CH), BF16),
            pltpu.VMEM((NCH, T, CH), BF16),
            pltpu.VMEM((NCH, 4, 16, CH), BF16),
            pltpu.VMEM((2, NCH, 4, 16, CH), BF16),
            pltpu.VMEM((4, 32, 128), F32),
            pltpu.VMEM((2, 4, 16, 128), BF16),
            pltpu.VMEM((2, 2, 4, 16, 128), BF16),
            pltpu.VMEM((4, 16, CH), F32),
            pltpu.VMEM((4, 32, 128), F32),
            pltpu.VMEM((T, CH), F32),
            pltpu.VMEM((T, CH), F32),
            pltpu.VMEM((T, CH), BF16),
            pltpu.VMEM((T, CH), BF16),
            pltpu.VMEM((T, D), F32),
            pltpu.VMEM((8, T, 128), F32),
            pltpu.VMEM((8 * T, 128), F32),
            pltpu.VMEM((T, D), BF16),
            pltpu.VMEM((4, npeer, 32, 128), BF16),
            pltpu.VMEM((4, npeer, 32, 128), BF16),
            pltpu.VMEM((T, D), BF16),
            pltpu.VMEM((T, D), F32),
            pltpu.VMEM((T, 3 * D), BF16),
            pltpu.VMEM((T, D), BF16),
            pltpu.VMEM((T, D), BF16),
            pltpu.VMEM((T, 3 * D), BF16),
            pltpu.VMEM((32, 128), F32),
            pltpu.VMEM((256, 128), F32),
            pltpu.VMEM((64, 256), F32),
            dma((4, NCH)),
            dma((2, NCH, 4)),
            dma((2, NCH, 4)),
            dma((2, 2, 4)),
            dma((2, 2, 4)),
            dma((4,)),
            dma((4,)),
            dma((4,)),
        ],
        compiler_params=pltpu.CompilerParams(
            collective_id=0, has_side_effects=True, vmem_limit_bytes=62 * 1024 * 1024
        ),
        cost_estimate=pl.CostEstimate(
            flops=13_000_000_000, bytes_accessed=27_000_000, transcendentals=5_000_000
        ),
    )(
        image,
        gain_conv,
        w_expand,
        kernel_taps,
        w_project,
        gain_attn.reshape(1, D),
        w_qkv,
        bias_table,
        w_out,
        cotangent.reshape(T, D),
    )
    rows = pl.BlockSpec((64, D), lambda i: (i, 0))
    out, dimg = pl.pallas_call(
        last_kernel,
        grid=(T // 64,),
        out_shape=(whole, whole),
        in_specs=[rows, pl.BlockSpec((1, D), lambda i: (0, 0)), rows, rows, rows],
        out_specs=(rows, rows),
    )(image, gain_conv, sent, d_normed, d_mid)
    return out.reshape(height, breadth, width), dimg.reshape(height, breadth, width)


def solution(mesh):
    whole = P("rows", "cols", None)
    return jax.shard_map(
        local,
        mesh=mesh,
        in_specs=(whole, P(), P(), P(), P(), P(), P(), P(), P(), whole),
        out_specs=(whole, whole),
        check_vma=False,
    )
```

```python
import jax
import jax.numpy as jnp
from jax import lax
from jax.experimental import pallas as pl
from jax.experimental.pallas import tpu as pltpu
from jax.sharding import PartitionSpec as P

F32 = jnp.float32
BF16 = jnp.bfloat16
MESH = pl.DeviceIdType.MESH
EPS = 1e-05
GRID = 8
T = 256
D = 1024
E = 4096
CH = 1024
NCH = E // CH
LT = CH // 128
QCH = 3 * D // CH
NT = (((1,), (1,)), ((), ()))


def dot_nt(a, b):
    return lax.dot_general(a, b, NT, preferred_element_type=F32)


def dot_nn(a, b):
    return jnp.dot(a, b, preferred_element_type=F32)


def gelu_parts(v):
    e = jnp.exp2(v * v * (-0.5 * 1.4426950408889634))
    u = 1.0 + jnp.abs(v) * (0.3275911 * 0.7071067811865476)
    t = pl.reciprocal(u, approx=True)
    t = t * (2.0 - u * t)
    poly = t * (0.5 * 1.061405429) + (0.5 * -1.453152027)
    poly = poly * t + (0.5 * 1.421413741)
    poly = poly * t + (0.5 * -0.284496736)
    poly = poly * t + (0.5 * 0.254829592)
    tail = poly * t * e
    cdf = jnp.where(v >= 0, 1.0 - tail, tail)
    return cdf, e * 0.3989422804014327


def norm_parts(x):
    c = x - jnp.mean(x, axis=-1, keepdims=True)
    r = lax.rsqrt(jnp.mean(c * c, axis=-1, keepdims=True) + EPS)
    return c * r, r

def norm_back(x, dy, gain):
    xh, r = norm_parts(x)
    dg = dy * gain
    m1 = jnp.mean(dg, axis=-1, keepdims=True)
    m2 = jnp.mean(dg * xh, axis=-1, keepdims=True)
    return (dg - m1 - xh * m2) * r


def to_messages(x):
    n = x.shape[0] // 8
    low = lax.broadcasted_iota(jnp.int32, (n, 8, 128), 1) < 4
    even, odd = [], []
    for m in range(4):
        a = x[:, 256 * m : 256 * m + 128].reshape(n, 8, 128)
        b = x[:, 256 * m + 128 : 256 * m + 256].reshape(n, 8, 128)
        even.append(jnp.where(low, a, pltpu.roll(b, 4, 1)))
        odd.append(jnp.where(low, pltpu.roll(a, 4, 1), b))
    even = jnp.concatenate(even, axis=1)
    odd = jnp.concatenate(odd, axis=1)
    return jnp.stack([even, odd], axis=1).reshape(2 * n, 32, 128)


def from_messages(x):
    n = x.shape[0] // 2
    low = lax.broadcasted_iota(jnp.int32, (n, 8, 128), 1) < 4
    pairs = x.reshape(n, 2, 32, 128)
    blocks = []
    for m in range(4):
        even = pairs[:, 0, 8 * m : 8 * m + 8]
        odd = pairs[:, 1, 8 * m : 8 * m + 8]
        blocks.append(jnp.where(low, even, pltpu.roll(odd, 4, 1)).reshape(8 * n, 128))
        blocks.append(jnp.where(low, pltpu.roll(even, 4, 1), odd).reshape(8 * n, 128))
    return jnp.concatenate(blocks, axis=1)


def kernel(
    img,
    gain_c,
    we,
    kern,
    wp,
    gain_a,
    wqkv,
    table,
    wo,
    cot,
    out,
    d_normed,
    d_mid,
    we_v,
    wp_v,
    wqkv_v,
    wo_v,
    wid,
    s1,
    s2,
    hs,
    hr,
    cs,
    csb,
    cr,
    hrf,
    crf,
    before_a,
    before_b,
    act_a,
    act_b,
    acc,
    xs,
    ys,
    na,
    send,
    recv,
    cotg,
    mg,
    qkv,
    datt,
    att,
    dqkv,
    tpad,
    wtab,
    btile,
    w_sem,
    hsend_sem,
    hrecv_sem,
    csend_sem,
    crecv_sem,
    asend_sem,
    arecv_sem,
    aown_sem,
):
    nrow = lax.axis_size("rows")
    ncol = lax.axis_size("cols")
    R = lax.axis_index("rows")
    C = lax.axis_index("cols")
    core = lax.rem(R, 2)
    me = (R // 2) * ncol + C
    npeer = (nrow // 2) * ncol

    def we_copy(k):
        return pltpu.make_async_copy(
            we.at[:, pl.ds(pl.multiple_of(k * CH, CH), CH)], we_v.at[k], w_sem.at[0, k]
        )

    def wp_copy(k):
        return pltpu.make_async_copy(
            wp.at[pl.ds(pl.multiple_of(k * CH, CH), CH), :], wp_v.at[k], w_sem.at[1, k]
        )

    def wqkv_copy(k):
        return pltpu.make_async_copy(
            wqkv.at[:, pl.ds(pl.multiple_of(k * CH, CH), CH)], wqkv_v.at[k], w_sem.at[2, k]
        )

    wo_copy = pltpu.make_async_copy(wo, wo_v, w_sem.at[3, 0])
    for k in range(NCH):
        we_copy(k).start()
    wo_copy.start()
    for k in range(NCH):
        wp_copy(k).start()
    for k in range(QCH):
        wqkv_copy(k).start()

    barrier = pltpu.get_barrier_semaphore()

    def peer_coord(d):
        return (2 * (d // ncol) + core, lax.rem(d, ncol))

    def greet(q, carry):
        pr, pc = peer_coord(lax.rem(me + q, npeer))
        pl.semaphore_signal(barrier, inc=1, device_id=(pr, pc), device_id_type=MESH)
        return carry

    lax.fori_loop(1, npeer, greet, 0)
    has_u = R > 0
    has_d = R < nrow - 1
    has_l = C > 0
    has_r = C < ncol - 1
    for dr, cond_r in ((-1, has_u), (1, has_d)):
        for dc, cond_c in ((-1, has_l), (0, None), (1, has_r)):
            cond = cond_r if cond_c is None else jnp.logical_and(cond_r, cond_c)

            @pl.when(cond)
            def _():
                pl.semaphore_signal(
                    barrier, inc=1, device_id=(R + dr, C + dc), device_id_type=MESH
                )

    sides = ((-1, 0, has_u), (1, 0, has_d), (0, -1, has_l), (0, 1, has_r))
    corners = (
        (-1, -1, jnp.logical_and(has_u, has_l)),
        (-1, 1, jnp.logical_and(has_u, has_r)),
        (1, -1, jnp.logical_and(has_d, has_l)),
        (1, 1, jnp.logical_and(has_d, has_r)),
    )
    for s, (_, _, cond) in enumerate(sides):

        @pl.when(jnp.logical_not(cond))
        def _():
            for way in range(2):
                hr[way, :, s] = jnp.zeros((NCH, 16, CH), BF16)

    for s, (_, _, cond) in enumerate(corners):

        @pl.when(jnp.logical_not(cond))
        def _():
            for way in range(2):
                cr[way, :, s] = jnp.zeros((2, 16, 128), BF16)

    def side_copy(way, k, s):
        dr, dc, _ = sides[s]
        return pltpu.make_async_remote_copy(
            src_ref=hs.at[k, s],
            dst_ref=hr.at[way, k, s ^ 1],
            send_sem=hsend_sem.at[way, k, s],
            recv_sem=hrecv_sem.at[way, k, s ^ 1],
            device_id=(R + dr, C + dc),
            device_id_type=MESH,
        )

    def side_recv(way, k, s):
        return pltpu.make_async_copy(hs.at[k, s], hr.at[way, k, s], hrecv_sem.at[way, k, s])

    def corner_copy(way, half, s):
        dr, dc, _ = corners[s]
        return pltpu.make_async_remote_copy(
            src_ref=csb.at[half, s],
            dst_ref=cr.at[way, half, 3 - s],
            send_sem=csend_sem.at[way, half, s],
            recv_sem=crecv_sem.at[way, half, 3 - s],
            device_id=(R + dr, C + dc),
            device_id_type=MESH,
        )

    def corner_recv(way, half, s):
        return pltpu.make_async_copy(
            csb.at[half, s], cr.at[way, half, s], crecv_sem.at[way, half, s]
        )

    def send_halos(way, k):
        for j in range(LT):
            lanes = slice(128 * j, 128 * j + 128)
            tile = LT * k + j
            hs[k, 0, :, lanes] = wid[tile, 0:16, :].astype(BF16)
            hs[k, 1, :, lanes] = wid[tile, T - 16 : T, :].astype(BF16)
            hs[k, 2, :, lanes] = wid[tile, pl.ds(0, 16, stride=16), :].astype(BF16)
            hs[k, 3, :, lanes] = wid[tile, pl.ds(15, 16, stride=16), :].astype(BF16)
            for s, row in enumerate((0, 15, T - 16, T - 1)):
                cs[s, tile : tile + 1, :] = wid[tile, row : row + 1, :]
        for s, (_, _, cond) in enumerate(sides):

            @pl.when(cond)
            def _():
                side_copy(way, k, s).start()

        if k % 2 == 1:
            half = k // 2
            for s, (_, _, cond) in enumerate(corners):
                csb[half, s] = cs[s, 16 * half : 16 * half + 16, :].astype(BF16)

                @pl.when(cond)
                def _():
                    corner_copy(way, half, s).start()

    def wait_halos(way, k):
        for s, (_, _, cond) in enumerate(sides):

            @pl.when(cond)
            def _():
                side_recv(way, k, s).wait()

        if k % 2 == 0:
            half = k // 2
            for s, (_, _, cond) in enumerate(corners):

                @pl.when(cond)
                def _():
                    corner_recv(way, half, s).wait()

                crf[s, 16 * half : 16 * half + 16, :] = cr[way, half, s].astype(F32)

        for s in range(4):
            hrf[s] = hr[way, k, s].astype(F32)

    def wait_halo_sends(way):
        def one(k, carry):
            for s, (_, _, cond) in enumerate(sides):

                @pl.when(cond)
                def _():
                    side_copy(way, k, s).wait_send()

            return carry

        lax.fori_loop(0, NCH, one, 0)
        for half in range(2):
            for s, (_, _, cond) in enumerate(corners):

                @pl.when(cond)
                def _():
                    corner_copy(way, half, s).wait_send()

    def a2a_start(n):
        def one(q, carry):
            d = lax.rem(me + q, npeer)
            pltpu.make_async_remote_copy(
                src_ref=send.at[n, d],
                dst_ref=recv.at[n, me],
                send_sem=asend_sem.at[n],
                recv_sem=arecv_sem.at[n],
                device_id=peer_coord(d),
                device_id_type=MESH,
            ).start()
            return carry

        lax.fori_loop(1, npeer, one, 0)
        pltpu.make_async_copy(send.at[n, me], recv.at[n, me], aown_sem.at[n]).start()

    def a2a_wait(n):
        part = pl.ds(0, npeer - 1)
        pltpu.make_async_copy(send.at[n, me], recv.at[n, me], aown_sem.at[n]).wait()
        pltpu.make_async_copy(send.at[n, part], recv.at[n, part], arecv_sem.at[n]).wait()

    def a2a_wait_send(n):
        part = pl.ds(0, npeer - 1)
        pltpu.make_async_copy(send.at[n, part], recv.at[n, part], asend_sem.at[n]).wait()

    def pack(n):
        def gather(b, carry):
            for t in range(4):
                ys[pl.ds(4 * b + t, 64, stride=32), :] = xs[b, pl.ds(64 * t, 64), :]
            return carry

        lax.fori_loop(0, 8, gather, 0)

        def narrow(d, carry):
            block = ys[pl.ds(pl.multiple_of(d * 256, 256), 256), :]
            send[n, pl.ds(d * 8, 8)] = block.reshape(8, 32, 128).astype(BF16)
            return carry

        lax.fori_loop(0, 8, narrow, 0)

    def unpack(n):
        def widen_rows(d, carry):
            block = recv[n, pl.ds(d * 8, 8)].astype(F32).reshape(256, 128)
            ys[pl.ds(pl.multiple_of(d * 256, 256), 256), :] = block
            return carry

        lax.fori_loop(0, 8, widen_rows, 0)

        def spread(b, carry):
            for t in range(4):
                xs[b, pl.ds(64 * t, 64), :] = ys[pl.ds(4 * b + t, 64, stride=32), :]
            return carry

        lax.fori_loop(0, 8, spread, 0)

    def blocks32(body):
        def one(i, carry):
            for u in range(2):
                at = i * 2 + u
                body(pl.ds(pl.multiple_of(at * 32, 32), 32), pl.ds(at * 8, 8))
            return carry

        lax.fori_loop(0, T // 64, one, 0)

    def put_xs(rows, value):
        for b in range(8):
            xs[b, rows, :] = value[:, 128 * b : 128 * b + 128]

    def get_xs(rows):
        return jnp.concatenate([xs[b, rows, :] for b in range(8)], axis=1)

    def put_wid(k, rows, value):
        for j in range(LT):
            wid[LT * k + j, rows, :] = value[:, 128 * j : 128 * j + 128]

    def tiles(body, size=32, together=4):
        def one(i, carry):
            for u in range(together):
                body(pl.ds(pl.multiple_of(i * (size * together) + u * size, size), size))
            return carry

        lax.fori_loop(0, T // (size * together), one, 0)

    def norm_in(rows, block):
        xh, _ = norm_parts(img[rows, :].astype(F32))
        na[rows, :] = (xh * gain_c[...]).astype(BF16)
        send[0, block] = to_messages(cot[rows, :].astype(F32)).astype(BF16)

    blocks32(norm_in)

    n_other = (has_u.astype(jnp.int32) + has_d.astype(jnp.int32)) * (
        1 + has_l.astype(jnp.int32) + has_r.astype(jnp.int32)
    )
    befores = (before_a, before_b)
    acts = (act_a, act_b)

    def widen(k):
        for i in range(T // 16):
            rows = slice(16 * i, 16 * i + 16)
            v = befores[k % 2][rows, :]
            cdf, pdf = gelu_parts(v)
            put_wid(k, rows, v * cdf)
            s1[k, rows, :] = (cdf + v * pdf).astype(BF16)

    for k in range(NCH + 1):
        if k < NCH:
            we_copy(k).wait()
            befores[k % 2][...] = dot_nn(na[...], we_v[k])
        if k >= 1:
            widen(k - 1)
            if k == 1:
                pl.semaphore_wait(barrier, npeer - 1 + n_other)
            send_halos(0, k - 1)
    a2a_start(0)

    iota16 = lax.broadcasted_iota(jnp.int32, (16, 128), 0)
    at_first = iota16 == 0
    at_last = iota16 == 15

    def conv(k, j, flip, done):
        lanes = slice(128 * j, 128 * j + 128)
        wide = slice(k * CH + 128 * j, k * CH + 128 * j + 128)
        w = [
            [kern[2 - a if flip else a, pl.ds(2 - b if flip else b, 1), wide] for b in range(3)]
            for a in range(3)
        ]
        sums = {}
        for r in range(-1, 17):
            if r == -1 or r == 16:
                low = r == 16
                x = hrf[1 if low else 0, :, lanes]
                cell = slice(LT * k + j, LT * k + j + 1)
                left = crf[2 if low else 0, cell, :]
                right = crf[3 if low else 1, cell, :]
            else:
                x = wid[LT * k + j, 16 * r : 16 * r + 16, :]
                left = hrf[2, r : r + 1, lanes]
                right = hrf[3, r : r + 1, lanes]
            xl = jnp.where(at_first, left, pltpu.roll(x, 1, 0))
            xr = jnp.where(at_last, right, pltpu.roll(x, 15, 0))
            for a in range(3):
                ro = r - a + 1
                if 0 <= ro < 16:
                    part = xl * w[a][0] + x * w[a][1] + xr * w[a][2]
                    sums[ro] = sums[ro] + part if ro in sums else part
            if r >= 1:
                done(r - 1, sums.pop(r - 1))

    for k in range(NCH + 1):
        if k >= 1:
            wp_copy(k - 1).wait()
        if k < NCH:
            wait_halos(0, k)
            for j in range(LT):
                lanes = slice(128 * j, 128 * j + 128)

                def done(r, v):
                    cdf, pdf = gelu_parts(v)
                    acts[k % 2][16 * r : 16 * r + 16, lanes] = (v * cdf).astype(BF16)
                    s2[k, 16 * r : 16 * r + 16, lanes] = (cdf + v * pdf).astype(BF16)

                conv(k, j, False, done)
        if k >= 1:
            part = dot_nn(acts[(k - 1) % 2][...], wp_v[k - 1])
            acc[...] = part if k == 1 else acc[...] + part

    def merge(rows, block):
        send[1, block] = to_messages(img[rows, :].astype(F32) + acc[rows, :]).astype(BF16)

    blocks32(merge)
    a2a_start(1)

    a2a_wait(0)
    unpack(0)

    def take_cot(rows):
        cotg[rows, :] = get_xs(rows).astype(BF16)

    tiles(take_cot)
    wo_copy.wait()
    for h in range(2):
        datt[:, 512 * h : 512 * h + 512] = dot_nt(
            cotg[...], wo_v[512 * h : 512 * h + 512, :]
        ).astype(BF16)

    tpad[...] = jnp.zeros((32, 128), F32)
    halves = [None, None]
    for di in range(15):
        tpad[:, 0:15] = table[:, di, :]
        moved = tpad[...]
        if di % 8:
            moved = pltpu.roll(moved, 16 * (di % 8), 1)
        old = halves[di // 8]
        halves[di // 8] = moved if old is None else old + moved
    tab = jnp.concatenate(halves, axis=1)
    tab_hi = tab.astype(BF16)
    rest = tab - tab_hi.astype(F32)
    tab_mid = rest.astype(BF16)
    tab_lo = (rest - tab_mid.astype(F32)).astype(BF16)
    lane = lax.broadcasted_iota(jnp.int32, (256, 128), 1)
    source = lax.broadcasted_iota(jnp.int32, (256, 128), 0)
    for jp in range(8):
        wanted = (lane // 8) * 16 + lax.rem(lane, 8) - jp + 7
        pick = jnp.where(source == wanted, 1.0, 0.0).astype(BF16)
        wtab[pl.ds(jp, 32, stride=8), :] = (
            dot_nn(tab_hi, pick) + dot_nn(tab_mid, pick) + dot_nn(tab_lo, pick)
        )

    lane8 = lax.broadcasted_iota(jnp.int32, (8, 128), 1)

    def lay_bias(quad, carry):
        for hp in range(2):
            wa = wtab[pl.ds(pl.multiple_of((4 * quad + 2 * hp) * 8, 8), 8), :]
            wb = wtab[pl.ds(pl.multiple_of((4 * quad + 2 * hp) * 8 + 8, 8), 8), :]
            for ip in range(8):
                s = (7 - ip) * 8
                first = pltpu.roll(wa, (128 - s) % 128, 1)
                second = pltpu.roll(wb, (192 - s) % 128, 1)
                btile[quad, 8 * ip : 8 * ip + 8, 128 * hp : 128 * hp + 128] = jnp.where(
                    lane8 < 64, first, second
                )
        return carry

    lax.fori_loop(0, 8, lay_bias, 0)
    wait_halo_sends(0)
    a2a_wait(1)
    unpack(1)

    def norm_mid(rows):
        x = get_xs(rows)
        mg[rows, :] = x
        xh, _ = norm_parts(x)
        na[rows, :] = (xh * gain_a[...]).astype(BF16)

    tiles(norm_mid)

    def make_qkv(k, carry):
        wqkv_copy(k).wait()
        qkv[:, pl.ds(pl.multiple_of(k * CH, CH), CH)] = dot_nn(na[...], wqkv_v[k]).astype(BF16)
        return carry

    lax.fori_loop(0, QCH, make_qkv, 0)

    scale = (D // 32) ** -0.5
    lane64 = lax.broadcasted_iota(jnp.int32, (64, 128), 1)
    masks = [(lane64 // 32 == h).astype(F32) for h in range(4)]
    masks16 = [m.astype(BF16) for m in masks]
    zero = jnp.zeros((64, 128), BF16)

    def stack_heads(x):
        return jnp.concatenate([x * m for m in masks16], axis=0)

    def attend(quad, carry):
        at = pl.multiple_of(quad * 128, 128)
        rows = [slice(64 * t, 64 * t + 64) for t in range(4)]
        kk = [qkv[r, pl.ds(D + at, 128)] for r in rows]
        vv = [qkv[r, pl.ds(2 * D + at, 128)] for r in rows]
        qm = [stack_heads(qkv[r, pl.ds(at, 128)]) for r in rows]
        dom = [stack_heads(datt[r, pl.ds(at, 128)]) for r in rows]
        score = [dot_nt(kk[t], qm[t]) for t in range(4)]
        dp = [dot_nt(vv[t], dom[t]) for t in range(4)]
        both = []
        for t in range(4):
            sc = score[t] * scale + btile[quad]
            p = jnp.exp(sc - jnp.max(sc, axis=0, keepdims=True))
            p = p * (1.0 / jnp.sum(p, axis=0, keepdims=True))
            ds = p * (dp[t] - jnp.sum(p * dp[t], axis=0, keepdims=True)) * scale
            both.append(jnp.concatenate([p, ds], axis=0))
        for t in range(4):
            turned = jnp.concatenate([dom[t], qm[t]], axis=1)
            d_both = dot_nn(both[t].astype(BF16), turned)
            dqkv[rows[t], pl.ds(D + at, 128)] = d_both[64:, 128:].astype(BF16)
            dqkv[rows[t], pl.ds(2 * D + at, 128)] = d_both[:64, :128].astype(BF16)
        turned = [b.T.astype(BF16) for b in both]
        big = []
        for t in range(4):
            upper = jnp.concatenate([vv[t], zero], axis=1)
            lower = jnp.concatenate([zero, kk[t]], axis=1)
            big.append(dot_nn(turned[t], jnp.concatenate([upper, lower], axis=0)))
        for t in range(4):
            parts = [big[t][64 * h : 64 * h + 64] for h in range(4)]
            o = sum(parts[h][:, :128] * masks[h] for h in range(4))
            dq = sum(parts[h][:, 128:] * masks[h] for h in range(4))
            att[rows[t], pl.ds(at, 128)] = o.astype(BF16)
            dqkv[rows[t], pl.ds(at, 128)] = dq.astype(BF16)
        return carry

    lax.fori_loop(0, 8, attend, 0)

    for h in range(2):
        cols = slice(512 * h, 512 * h + 512)
        acc[:, cols] = mg[:, cols] + dot_nn(att[...], wo_v[:, cols])
    tiles(lambda rows: put_xs(rows, acc[rows, :]))
    pack(2)
    a2a_start(2)

    def back_qkv(k):
        part = dot_nt(dqkv[:, CH * k : CH * k + CH], wqkv_v[k])
        acc[...] = part if k == 0 else acc[...] + part

    for k in range(QCH):
        back_qkv(k)

    def norm_mid_back(rows):
        dy = acc[rows, :].astype(BF16).astype(F32)
        dx = norm_back(mg[rows, :], dy, gain_a[...]).astype(BF16).astype(F32)
        put_xs(rows, cotg[rows, :].astype(F32) + dx)

    tiles(norm_mid_back)
    pack(3)
    a2a_start(3)

    a2a_wait(2)

    def take_out(rows, block):
        out[rows, :] = from_messages(recv[2, block].astype(F32)).astype(BF16)

    blocks32(take_out)
    a2a_wait(3)

    def take_dm(rows, block):
        na[rows, :] = from_messages(recv[3, block].astype(F32)).astype(BF16)

    blocks32(take_dm)

    def slope(k):
        for i in range(T // 16):
            rows = slice(16 * i, 16 * i + 16)
            put_wid(k, rows, befores[k % 2][rows, :] * s2[k, rows, :].astype(F32))

    for k in range(NCH + 1):
        if k < NCH:
            befores[k % 2][...] = dot_nt(na[...], wp_v[k])
        if k >= 1:
            slope(k - 1)
            send_halos(1, k - 1)

    for k in range(NCH + 1):
        if k < NCH:
            wait_halos(1, k)
            for j in range(LT):
                lanes = slice(128 * j, 128 * j + 128)

                def done(r, v):
                    back = s1[k, 16 * r : 16 * r + 16, lanes].astype(F32)
                    acts[k % 2][16 * r : 16 * r + 16, lanes] = (v * back).astype(BF16)

                conv(k, j, True, done)
        if k >= 1:
            part = dot_nt(acts[(k - 1) % 2][...], we_v[k - 1])
            acc[...] = part if k == 1 else acc[...] + part

    def finish(rows):
        d_normed[rows, :] = acc[rows, :].astype(BF16)
        d_mid[rows, :] = na[rows, :]

    tiles(finish)
    wait_halo_sends(1)
    for n in range(4):
        a2a_wait_send(n)


def last_kernel(img, gain_c, sent, d_normed, d_mid, out, dimg):
    out[...] = sent[...]
    dy = d_normed[...].astype(F32)
    dx = norm_back(img[...].astype(F32), dy, gain_c[...]).astype(BF16).astype(F32)
    dimg[...] = (d_mid[...].astype(F32) + dx).astype(BF16)


def local(
    image, gain_conv, w_expand, kernel_taps, w_project, gain_attn, w_qkv, bias_table, w_out, cotangent
):
    height, breadth, width = image.shape
    vmem = pl.BlockSpec(memory_space=pltpu.VMEM)
    hbm = pl.BlockSpec(memory_space=pl.ANY)
    dma = pltpu.SemaphoreType.DMA
    npeer = 64
    image = image.reshape(T, D)
    gain_conv = gain_conv.reshape(1, D)
    whole = jax.ShapeDtypeStruct((T, D), BF16)
    sent, d_normed, d_mid = pl.pallas_call(
        kernel,
        out_shape=(whole, whole, whole),
        in_specs=[vmem, vmem, hbm, vmem, hbm, vmem, hbm, vmem, hbm, vmem],
        out_specs=(vmem, vmem, vmem),
        scratch_shapes=[
            pltpu.VMEM((NCH, D, CH), BF16),
            pltpu.VMEM((NCH, CH, D), BF16),
            pltpu.VMEM((QCH, D, CH), BF16),
            pltpu.VMEM((D, D), BF16),
            pltpu.VMEM((NCH * CH // 128, T, 128), F32),
            pltpu.VMEM((NCH, T, CH), BF16),
            pltpu.VMEM((NCH, T, CH), BF16),
            pltpu.VMEM((NCH, 4, 16, CH), BF16),
            pltpu.VMEM((2, NCH, 4, 16, CH), BF16),
            pltpu.VMEM((4, 32, 128), F32),
            pltpu.VMEM((2, 4, 16, 128), BF16),
            pltpu.VMEM((2, 2, 4, 16, 128), BF16),
            pltpu.VMEM((4, 16, CH), F32),
            pltpu.VMEM((4, 32, 128), F32),
            pltpu.VMEM((T, CH), F32),
            pltpu.VMEM((T, CH), F32),
            pltpu.VMEM((T, CH), BF16),
            pltpu.VMEM((T, CH), BF16),
            pltpu.VMEM((T, D), F32),
            pltpu.VMEM((8, T, 128), F32),
            pltpu.VMEM((8 * T, 128), F32),
            pltpu.VMEM((T, D), BF16),
            pltpu.VMEM((4, npeer, 32, 128), BF16),
            pltpu.VMEM((4, npeer, 32, 128), BF16),
            pltpu.VMEM((T, D), BF16),
            pltpu.VMEM((T, D), F32),
            pltpu.VMEM((T, 3 * D), BF16),
            pltpu.VMEM((T, D), BF16),
            pltpu.VMEM((T, D), BF16),
            pltpu.VMEM((T, 3 * D), BF16),
            pltpu.VMEM((32, 128), F32),
            pltpu.VMEM((256, 128), F32),
            pltpu.VMEM((8, 64, 256), F32),
            dma((4, NCH)),
            dma((2, NCH, 4)),
            dma((2, NCH, 4)),
            dma((2, 2, 4)),
            dma((2, 2, 4)),
            dma((4,)),
            dma((4,)),
            dma((4,)),
        ],
        compiler_params=pltpu.CompilerParams(
            collective_id=0, has_side_effects=True, vmem_limit_bytes=62 * 1024 * 1024
        ),
        cost_estimate=pl.CostEstimate(
            flops=13_000_000_000, bytes_accessed=27_000_000, transcendentals=5_000_000
        ),
    )(
        image,
        gain_conv,
        w_expand,
        kernel_taps,
        w_project,
        gain_attn.reshape(1, D),
        w_qkv,
        bias_table,
        w_out,
        cotangent.reshape(T, D),
    )
    rows = pl.BlockSpec((64, D), lambda i: (i, 0))
    out, dimg = pl.pallas_call(
        last_kernel,
        grid=(T // 64,),
        out_shape=(whole, whole),
        in_specs=[rows, pl.BlockSpec((1, D), lambda i: (0, 0)), rows, rows, rows],
        out_specs=(rows, rows),
    )(image, gain_conv, sent, d_normed, d_mid)
    return out.reshape(height, breadth, width), dimg.reshape(height, breadth, width)


def solution(mesh):
    whole = P("rows", "cols", None)
    return jax.shard_map(
        local,
        mesh=mesh,
        in_specs=(whole, P(), P(), P(), P(), P(), P(), P(), P(), whole),
        out_specs=(whole, whole),
        check_vma=False,
    )
```

```python
import jax
import jax.numpy as jnp
from jax import lax
from jax.experimental import pallas as pl
from jax.experimental.pallas import tpu as pltpu
from jax.sharding import PartitionSpec as P

F32 = jnp.float32
BF16 = jnp.bfloat16
MESH = pl.DeviceIdType.MESH
EPS = 1e-05
GRID = 8
T = 256
D = 1024
E = 4096
CH = 1024
NCH = E // CH
LT = CH // 128
QCH = 3 * D // CH
NT = (((1,), (1,)), ((), ()))


def dot_nt(a, b):
    return lax.dot_general(a, b, NT, preferred_element_type=F32)


def dot_nn(a, b):
    return jnp.dot(a, b, preferred_element_type=F32)


def gelu_parts(v):
    e = jnp.exp2(v * v * (-0.5 * 1.4426950408889634))
    u = 1.0 + jnp.abs(v) * (0.3275911 * 0.7071067811865476)
    t = pl.reciprocal(u, approx=True)
    t = t * (2.0 - u * t)
    poly = t * (0.5 * 1.061405429) + (0.5 * -1.453152027)
    poly = poly * t + (0.5 * 1.421413741)
    poly = poly * t + (0.5 * -0.284496736)
    poly = poly * t + (0.5 * 0.254829592)
    tail = poly * t * e
    cdf = jnp.where(v >= 0, 1.0 - tail, tail)
    return cdf, e * 0.3989422804014327


def norm_parts(x):
    c = x - jnp.mean(x, axis=-1, keepdims=True)
    r = lax.rsqrt(jnp.mean(c * c, axis=-1, keepdims=True) + EPS)
    return c * r, r

def norm_back(x, dy, gain):
    xh, r = norm_parts(x)
    dg = dy * gain
    m1 = jnp.mean(dg, axis=-1, keepdims=True)
    m2 = jnp.mean(dg * xh, axis=-1, keepdims=True)
    return (dg - m1 - xh * m2) * r


def to_messages(x):
    n = x.shape[0] // 8
    low = lax.broadcasted_iota(jnp.int32, (n, 8, 128), 1) < 4
    even, odd = [], []
    for m in range(4):
        a = x[:, 256 * m : 256 * m + 128].reshape(n, 8, 128)
        b = x[:, 256 * m + 128 : 256 * m + 256].reshape(n, 8, 128)
        even.append(jnp.where(low, a, pltpu.roll(b, 4, 1)))
        odd.append(jnp.where(low, pltpu.roll(a, 4, 1), b))
    even = jnp.concatenate(even, axis=1)
    odd = jnp.concatenate(odd, axis=1)
    return jnp.stack([even, odd], axis=1).reshape(2 * n, 32, 128)


def from_messages(x):
    n = x.shape[0] // 2
    low = lax.broadcasted_iota(jnp.int32, (n, 8, 128), 1) < 4
    pairs = x.reshape(n, 2, 32, 128)
    blocks = []
    for m in range(4):
        even = pairs[:, 0, 8 * m : 8 * m + 8]
        odd = pairs[:, 1, 8 * m : 8 * m + 8]
        blocks.append(jnp.where(low, even, pltpu.roll(odd, 4, 1)).reshape(8 * n, 128))
        blocks.append(jnp.where(low, pltpu.roll(even, 4, 1), odd).reshape(8 * n, 128))
    return jnp.concatenate(blocks, axis=1)


def kernel(
    img,
    gain_c,
    we,
    kern,
    wp,
    gain_a,
    wqkv,
    table,
    wo,
    cot,
    out,
    d_normed,
    d_mid,
    we_v,
    wp_v,
    wqkv_v,
    wo_v,
    wid,
    s1,
    s2,
    hs,
    hr,
    cs,
    csb,
    cr,
    hrf,
    crf,
    before_a,
    before_b,
    act_a,
    act_b,
    acc,
    ys,
    na,
    send,
    recv,
    cotg,
    mg,
    qkv,
    datt,
    att,
    dqkv,
    tpad,
    wtab,
    btile,
    w_sem,
    hsend_sem,
    hrecv_sem,
    csend_sem,
    crecv_sem,
    asend_sem,
    arecv_sem,
    aown_sem,
):
    nrow = lax.axis_size("rows")
    ncol = lax.axis_size("cols")
    R = lax.axis_index("rows")
    C = lax.axis_index("cols")
    core = lax.rem(R, 2)
    me = (R // 2) * ncol + C
    npeer = (nrow // 2) * ncol

    def we_copy(k):
        return pltpu.make_async_copy(
            we.at[:, pl.ds(pl.multiple_of(k * CH, CH), CH)], we_v.at[k], w_sem.at[0, k]
        )

    def wp_copy(k):
        return pltpu.make_async_copy(
            wp.at[pl.ds(pl.multiple_of(k * CH, CH), CH), :], wp_v.at[k], w_sem.at[1, k]
        )

    def wqkv_copy(k):
        return pltpu.make_async_copy(
            wqkv.at[:, pl.ds(pl.multiple_of(k * CH, CH), CH)], wqkv_v.at[k], w_sem.at[2, k]
        )

    wo_copy = pltpu.make_async_copy(wo, wo_v, w_sem.at[3, 0])
    for k in range(NCH):
        we_copy(k).start()
    wo_copy.start()
    for k in range(NCH):
        wp_copy(k).start()
    for k in range(QCH):
        wqkv_copy(k).start()

    barrier = pltpu.get_barrier_semaphore()

    def peer_coord(d):
        return (2 * (d // ncol) + core, lax.rem(d, ncol))

    def greet(q, carry):
        pr, pc = peer_coord(lax.rem(me + q, npeer))
        pl.semaphore_signal(barrier, inc=1, device_id=(pr, pc), device_id_type=MESH)
        return carry

    lax.fori_loop(1, npeer, greet, 0)
    has_u = R > 0
    has_d = R < nrow - 1
    has_l = C > 0
    has_r = C < ncol - 1
    for dr, cond_r in ((-1, has_u), (1, has_d)):
        for dc, cond_c in ((-1, has_l), (0, None), (1, has_r)):
            cond = cond_r if cond_c is None else jnp.logical_and(cond_r, cond_c)

            @pl.when(cond)
            def _():
                pl.semaphore_signal(
                    barrier, inc=1, device_id=(R + dr, C + dc), device_id_type=MESH
                )

    sides = ((-1, 0, has_u), (1, 0, has_d), (0, -1, has_l), (0, 1, has_r))
    corners = (
        (-1, -1, jnp.logical_and(has_u, has_l)),
        (-1, 1, jnp.logical_and(has_u, has_r)),
        (1, -1, jnp.logical_and(has_d, has_l)),
        (1, 1, jnp.logical_and(has_d, has_r)),
    )
    for s, (_, _, cond) in enumerate(sides):

        @pl.when(jnp.logical_not(cond))
        def _():
            for way in range(2):
                hr[way, :, s] = jnp.zeros((NCH, 16, CH), BF16)

    for s, (_, _, cond) in enumerate(corners):

        @pl.when(jnp.logical_not(cond))
        def _():
            for way in range(2):
                cr[way, :, s] = jnp.zeros((2, 16, 128), BF16)

    def side_copy(way, k, s):
        dr, dc, _ = sides[s]
        return pltpu.make_async_remote_copy(
            src_ref=hs.at[k, s],
            dst_ref=hr.at[way, k, s ^ 1],
            send_sem=hsend_sem.at[way, k, s],
            recv_sem=hrecv_sem.at[way, k, s ^ 1],
            device_id=(R + dr, C + dc),
            device_id_type=MESH,
        )

    def side_recv(way, k, s):
        return pltpu.make_async_copy(hs.at[k, s], hr.at[way, k, s], hrecv_sem.at[way, k, s])

    def corner_copy(way, half, s):
        dr, dc, _ = corners[s]
        return pltpu.make_async_remote_copy(
            src_ref=csb.at[half, s],
            dst_ref=cr.at[way, half, 3 - s],
            send_sem=csend_sem.at[way, half, s],
            recv_sem=crecv_sem.at[way, half, 3 - s],
            device_id=(R + dr, C + dc),
            device_id_type=MESH,
        )

    def corner_recv(way, half, s):
        return pltpu.make_async_copy(
            csb.at[half, s], cr.at[way, half, s], crecv_sem.at[way, half, s]
        )

    def send_halos(way, k):
        for j in range(LT):
            lanes = slice(128 * j, 128 * j + 128)
            tile = LT * k + j
            hs[k, 0, :, lanes] = wid[tile, 0:16, :].astype(BF16)
            hs[k, 1, :, lanes] = wid[tile, T - 16 : T, :].astype(BF16)
            hs[k, 2, :, lanes] = wid[tile, pl.ds(0, 16, stride=16), :].astype(BF16)
            hs[k, 3, :, lanes] = wid[tile, pl.ds(15, 16, stride=16), :].astype(BF16)
            for s, row in enumerate((0, 15, T - 16, T - 1)):
                cs[s, tile : tile + 1, :] = wid[tile, row : row + 1, :]
        for s, (_, _, cond) in enumerate(sides):

            @pl.when(cond)
            def _():
                side_copy(way, k, s).start()

        if k % 2 == 1:
            half = k // 2
            for s, (_, _, cond) in enumerate(corners):
                csb[half, s] = cs[s, 16 * half : 16 * half + 16, :].astype(BF16)

                @pl.when(cond)
                def _():
                    corner_copy(way, half, s).start()

    def wait_halos(way, k):
        for s, (_, _, cond) in enumerate(sides):

            @pl.when(cond)
            def _():
                side_recv(way, k, s).wait()

        if k % 2 == 0:
            half = k // 2
            for s, (_, _, cond) in enumerate(corners):

                @pl.when(cond)
                def _():
                    corner_recv(way, half, s).wait()

                crf[s, 16 * half : 16 * half + 16, :] = cr[way, half, s].astype(F32)

        for s in range(4):
            hrf[s] = hr[way, k, s].astype(F32)

    def wait_halo_sends(way):
        def one(k, carry):
            for s, (_, _, cond) in enumerate(sides):

                @pl.when(cond)
                def _():
                    side_copy(way, k, s).wait_send()

            return carry

        lax.fori_loop(0, NCH, one, 0)
        for half in range(2):
            for s, (_, _, cond) in enumerate(corners):

                @pl.when(cond)
                def _():
                    corner_copy(way, half, s).wait_send()

    def a2a_start(n):
        def one(q, carry):
            d = lax.rem(me + q, npeer)
            pltpu.make_async_remote_copy(
                src_ref=send.at[n, d],
                dst_ref=recv.at[n, me],
                send_sem=asend_sem.at[n],
                recv_sem=arecv_sem.at[n],
                device_id=peer_coord(d),
                device_id_type=MESH,
            ).start()
            return carry

        lax.fori_loop(1, npeer, one, 0)
        pltpu.make_async_copy(send.at[n, me], recv.at[n, me], aown_sem.at[n]).start()

    def a2a_wait(n):
        part = pl.ds(0, npeer - 1)
        pltpu.make_async_copy(send.at[n, me], recv.at[n, me], aown_sem.at[n]).wait()
        pltpu.make_async_copy(send.at[n, part], recv.at[n, part], arecv_sem.at[n]).wait()

    def a2a_wait_send(n):
        part = pl.ds(0, npeer - 1)
        pltpu.make_async_copy(send.at[n, part], recv.at[n, part], asend_sem.at[n]).wait()

    def pack(n):
        def narrow(d, carry):
            block = ys[pl.ds(pl.multiple_of(d * 256, 256), 256), :]
            send[n, pl.ds(d * 8, 8)] = block.reshape(8, 32, 128).astype(BF16)
            return carry

        lax.fori_loop(0, 8, narrow, 0)

    def unpack(n):
        def widen_rows(d, carry):
            block = recv[n, pl.ds(d * 8, 8)].astype(F32).reshape(256, 128)
            ys[pl.ds(pl.multiple_of(d * 256, 256), 256), :] = block
            return carry

        lax.fori_loop(0, 8, widen_rows, 0)

    def blocks32(body):
        def one(i, carry):
            for u in range(2):
                at = i * 2 + u
                body(pl.ds(pl.multiple_of(at * 32, 32), 32), pl.ds(at * 8, 8))
            return carry

        lax.fori_loop(0, T // 64, one, 0)

    def put_rows(start, value):
        for b in range(8):
            ys[pl.ds(start + 4 * b, 32, stride=32), :] = value[:, 128 * b : 128 * b + 128]

    def take_rows(start):
        return jnp.concatenate([ys[pl.ds(start + 4 * b, 32, stride=32), :] for b in range(8)], axis=1)

    def put_wid(k, rows, value):
        for j in range(LT):
            wid[LT * k + j, rows, :] = value[:, 128 * j : 128 * j + 128]

    def tiles(body):
        def one(i, carry):
            for u in range(4):
                rows = pl.ds(pl.multiple_of(i * 128 + u * 32, 32), 32)
                body(rows, 1024 * (u % 2) + 2 * i + u // 2)
            return carry

        lax.fori_loop(0, T // 128, one, 0)

    def norm_in(rows, block):
        xh, _ = norm_parts(img[rows, :].astype(F32))
        na[rows, :] = (xh * gain_c[...]).astype(BF16)
        send[0, block] = to_messages(cot[rows, :].astype(F32)).astype(BF16)

    blocks32(norm_in)

    n_other = (has_u.astype(jnp.int32) + has_d.astype(jnp.int32)) * (
        1 + has_l.astype(jnp.int32) + has_r.astype(jnp.int32)
    )
    befores = (before_a, before_b)
    acts = (act_a, act_b)

    def widen(k):
        for i in range(T // 16):
            rows = slice(16 * i, 16 * i + 16)
            v = befores[k % 2][rows, :]
            cdf, pdf = gelu_parts(v)
            put_wid(k, rows, v * cdf)
            s1[k, rows, :] = (cdf + v * pdf).astype(BF16)

    for k in range(NCH + 1):
        if k < NCH:
            we_copy(k).wait()
            befores[k % 2][...] = dot_nn(na[...], we_v[k])
        if k >= 1:
            widen(k - 1)
            if k == 1:
                pl.semaphore_wait(barrier, npeer - 1 + n_other)
            send_halos(0, k - 1)
    a2a_start(0)

    iota16 = lax.broadcasted_iota(jnp.int32, (16, 128), 0)
    at_first = iota16 == 0
    at_last = iota16 == 15

    def conv(k, j, flip, done):
        lanes = slice(128 * j, 128 * j + 128)
        wide = slice(k * CH + 128 * j, k * CH + 128 * j + 128)
        w = [
            [kern[2 - a if flip else a, pl.ds(2 - b if flip else b, 1), wide] for b in range(3)]
            for a in range(3)
        ]
        sums = {}
        for r in range(-1, 17):
            if r == -1 or r == 16:
                low = r == 16
                x = hrf[1 if low else 0, :, lanes]
                cell = slice(LT * k + j, LT * k + j + 1)
                left = crf[2 if low else 0, cell, :]
                right = crf[3 if low else 1, cell, :]
            else:
                x = wid[LT * k + j, 16 * r : 16 * r + 16, :]
                left = hrf[2, r : r + 1, lanes]
                right = hrf[3, r : r + 1, lanes]
            xl = jnp.where(at_first, left, pltpu.roll(x, 1, 0))
            xr = jnp.where(at_last, right, pltpu.roll(x, 15, 0))
            for a in range(3):
                ro = r - a + 1
                if 0 <= ro < 16:
                    part = xl * w[a][0] + x * w[a][1] + xr * w[a][2]
                    sums[ro] = sums[ro] + part if ro in sums else part
            if r >= 1:
                done(r - 1, sums.pop(r - 1))

    for k in range(NCH + 1):
        if k >= 1:
            wp_copy(k - 1).wait()
        if k < NCH:
            wait_halos(0, k)
            for j in range(LT):
                lanes = slice(128 * j, 128 * j + 128)

                def done(r, v):
                    cdf, pdf = gelu_parts(v)
                    acts[k % 2][16 * r : 16 * r + 16, lanes] = (v * cdf).astype(BF16)
                    s2[k, 16 * r : 16 * r + 16, lanes] = (cdf + v * pdf).astype(BF16)

                conv(k, j, False, done)
        if k >= 1:
            part = dot_nn(acts[(k - 1) % 2][...], wp_v[k - 1])
            acc[...] = part if k == 1 else acc[...] + part

    def merge(rows, block):
        send[1, block] = to_messages(img[rows, :].astype(F32) + acc[rows, :]).astype(BF16)

    blocks32(merge)
    a2a_start(1)

    a2a_wait(0)
    unpack(0)

    def take_cot(rows, start):
        cotg[rows, :] = take_rows(start).astype(BF16)

    tiles(take_cot)
    wo_copy.wait()
    for h in range(2):
        datt[:, 512 * h : 512 * h + 512] = dot_nt(
            cotg[...], wo_v[512 * h : 512 * h + 512, :]
        ).astype(BF16)

    tpad[...] = jnp.zeros((32, 128), F32)
    halves = [None, None]
    for di in range(15):
        tpad[:, 0:15] = table[:, di, :]
        moved = tpad[...]
        if di % 8:
            moved = pltpu.roll(moved, 16 * (di % 8), 1)
        old = halves[di // 8]
        halves[di // 8] = moved if old is None else old + moved
    tab = jnp.concatenate(halves, axis=1)
    tab_hi = tab.astype(BF16)
    rest = tab - tab_hi.astype(F32)
    tab_mid = rest.astype(BF16)
    tab_lo = (rest - tab_mid.astype(F32)).astype(BF16)
    lane = lax.broadcasted_iota(jnp.int32, (256, 128), 1)
    source = lax.broadcasted_iota(jnp.int32, (256, 128), 0)
    for jp in range(8):
        wanted = (lane // 8) * 16 + lax.rem(lane, 8) - jp + 7
        pick = jnp.where(source == wanted, 1.0, 0.0).astype(BF16)
        wtab[pl.ds(jp, 32, stride=8), :] = (
            dot_nn(tab_hi, pick) + dot_nn(tab_mid, pick) + dot_nn(tab_lo, pick)
        )

    lane8 = lax.broadcasted_iota(jnp.int32, (8, 128), 1)

    def lay_bias(quad, carry):
        for hp in range(2):
            wa = wtab[pl.ds(pl.multiple_of((4 * quad + 2 * hp) * 8, 8), 8), :]
            wb = wtab[pl.ds(pl.multiple_of((4 * quad + 2 * hp) * 8 + 8, 8), 8), :]
            for ip in range(8):
                s = (7 - ip) * 8
                first = pltpu.roll(wa, (128 - s) % 128, 1)
                second = pltpu.roll(wb, (192 - s) % 128, 1)
                btile[quad, 8 * ip : 8 * ip + 8, 128 * hp : 128 * hp + 128] = jnp.where(
                    lane8 < 64, first, second
                )
        return carry

    lax.fori_loop(0, 8, lay_bias, 0)
    wait_halo_sends(0)
    a2a_wait(1)
    unpack(1)

    def norm_mid(rows, start):
        x = take_rows(start)
        mg[rows, :] = x
        xh, _ = norm_parts(x)
        na[rows, :] = (xh * gain_a[...]).astype(BF16)

    tiles(norm_mid)

    def make_qkv(k, carry):
        wqkv_copy(k).wait()
        qkv[:, pl.ds(pl.multiple_of(k * CH, CH), CH)] = dot_nn(na[...], wqkv_v[k]).astype(BF16)
        return carry

    lax.fori_loop(0, QCH, make_qkv, 0)

    scale = (D // 32) ** -0.5
    lane64 = lax.broadcasted_iota(jnp.int32, (64, 128), 1)
    masks = [(lane64 // 32 == h).astype(F32) for h in range(4)]
    masks16 = [m.astype(BF16) for m in masks]
    zero = jnp.zeros((64, 128), BF16)

    def stack_heads(x):
        return jnp.concatenate([x * m for m in masks16], axis=0)

    def attend(quad, carry):
        at = pl.multiple_of(quad * 128, 128)
        rows = [slice(64 * t, 64 * t + 64) for t in range(4)]
        kk = [qkv[r, pl.ds(D + at, 128)] for r in rows]
        vv = [qkv[r, pl.ds(2 * D + at, 128)] for r in rows]
        qm = [stack_heads(qkv[r, pl.ds(at, 128)]) for r in rows]
        dom = [stack_heads(datt[r, pl.ds(at, 128)]) for r in rows]
        score = [dot_nt(kk[t], qm[t]) for t in range(4)]
        dp = [dot_nt(vv[t], dom[t]) for t in range(4)]
        both = []
        for t in range(4):
            sc = score[t] * scale + btile[quad]
            p = jnp.exp(sc - jnp.max(sc, axis=0, keepdims=True))
            p = p * (1.0 / jnp.sum(p, axis=0, keepdims=True))
            ds = p * (dp[t] - jnp.sum(p * dp[t], axis=0, keepdims=True)) * scale
            both.append(jnp.concatenate([p, ds], axis=0))
        for t in range(4):
            turned = jnp.concatenate([dom[t], qm[t]], axis=1)
            d_both = dot_nn(both[t].astype(BF16), turned)
            dqkv[rows[t], pl.ds(D + at, 128)] = d_both[64:, 128:].astype(BF16)
            dqkv[rows[t], pl.ds(2 * D + at, 128)] = d_both[:64, :128].astype(BF16)
        turned = [b.T.astype(BF16) for b in both]
        big = []
        for t in range(4):
            upper = jnp.concatenate([vv[t], zero], axis=1)
            lower = jnp.concatenate([zero, kk[t]], axis=1)
            big.append(dot_nn(turned[t], jnp.concatenate([upper, lower], axis=0)))
        for t in range(4):
            parts = [big[t][64 * h : 64 * h + 64] for h in range(4)]
            o = sum(parts[h][:, :128] * masks[h] for h in range(4))
            dq = sum(parts[h][:, 128:] * masks[h] for h in range(4))
            att[rows[t], pl.ds(at, 128)] = o.astype(BF16)
            dqkv[rows[t], pl.ds(at, 128)] = dq.astype(BF16)
        return carry

    lax.fori_loop(0, 8, attend, 0)

    def back_qkv(k):
        part = dot_nt(dqkv[:, CH * k : CH * k + CH], wqkv_v[k])
        acc[...] = part if k == 0 else acc[...] + part

    for k in range(QCH):
        back_qkv(k)

    def norm_mid_back(rows, start):
        dy = acc[rows, :].astype(BF16).astype(F32)
        dx = norm_back(mg[rows, :], dy, gain_a[...]).astype(BF16).astype(F32)
        put_rows(start, cotg[rows, :].astype(F32) + dx)

    tiles(norm_mid_back)
    pack(3)
    a2a_start(3)

    for h in range(2):
        cols = slice(512 * h, 512 * h + 512)
        acc[:, cols] = mg[:, cols] + dot_nn(att[...], wo_v[:, cols])

    def put_result(rows, start):
        put_rows(start, acc[rows, :])

    tiles(put_result)
    pack(2)
    a2a_start(2)
    a2a_wait(3)

    def take_dm(rows, block):
        na[rows, :] = from_messages(recv[3, block].astype(F32)).astype(BF16)

    blocks32(take_dm)

    def slope(k):
        for i in range(T // 16):
            rows = slice(16 * i, 16 * i + 16)
            put_wid(k, rows, befores[k % 2][rows, :] * s2[k, rows, :].astype(F32))

    for k in range(NCH + 1):
        if k < NCH:
            befores[k % 2][...] = dot_nt(na[...], wp_v[k])
        if k >= 1:
            slope(k - 1)
            send_halos(1, k - 1)

    a2a_wait(2)

    def take_out(rows, block):
        out[rows, :] = from_messages(recv[2, block].astype(F32)).astype(BF16)

    blocks32(take_out)

    for k in range(NCH + 1):
        if k < NCH:
            wait_halos(1, k)
            for j in range(LT):
                lanes = slice(128 * j, 128 * j + 128)

                def done(r, v):
                    back = s1[k, 16 * r : 16 * r + 16, lanes].astype(F32)
                    acts[k % 2][16 * r : 16 * r + 16, lanes] = (v * back).astype(BF16)

                conv(k, j, True, done)
        if k >= 1:
            part = dot_nt(acts[(k - 1) % 2][...], we_v[k - 1])
            acc[...] = part if k == 1 else acc[...] + part

    def finish(rows, start):
        d_normed[rows, :] = acc[rows, :].astype(BF16)
        d_mid[rows, :] = na[rows, :]

    tiles(finish)
    wait_halo_sends(1)
    for n in range(4):
        a2a_wait_send(n)


def last_kernel(img, gain_c, sent, d_normed, d_mid, out, dimg):
    out[...] = sent[...]
    dy = d_normed[...].astype(F32)
    dx = norm_back(img[...].astype(F32), dy, gain_c[...]).astype(BF16).astype(F32)
    dimg[...] = (d_mid[...].astype(F32) + dx).astype(BF16)


def local(
    image, gain_conv, w_expand, kernel_taps, w_project, gain_attn, w_qkv, bias_table, w_out, cotangent
):
    height, breadth, width = image.shape
    vmem = pl.BlockSpec(memory_space=pltpu.VMEM)
    hbm = pl.BlockSpec(memory_space=pl.ANY)
    dma = pltpu.SemaphoreType.DMA
    npeer = 64
    image = image.reshape(T, D)
    gain_conv = gain_conv.reshape(1, D)
    whole = jax.ShapeDtypeStruct((T, D), BF16)
    sent, d_normed, d_mid = pl.pallas_call(
        kernel,
        out_shape=(whole, whole, whole),
        in_specs=[vmem, vmem, hbm, vmem, hbm, vmem, hbm, vmem, hbm, vmem],
        out_specs=(vmem, vmem, vmem),
        scratch_shapes=[
            pltpu.VMEM((NCH, D, CH), BF16),
            pltpu.VMEM((NCH, CH, D), BF16),
            pltpu.VMEM((QCH, D, CH), BF16),
            pltpu.VMEM((D, D), BF16),
            pltpu.VMEM((NCH * CH // 128, T, 128), F32),
            pltpu.VMEM((NCH, T, CH), BF16),
            pltpu.VMEM((NCH, T, CH), BF16),
            pltpu.VMEM((NCH, 4, 16, CH), BF16),
            pltpu.VMEM((2, NCH, 4, 16, CH), BF16),
            pltpu.VMEM((4, 32, 128), F32),
            pltpu.VMEM((2, 4, 16, 128), BF16),
            pltpu.VMEM((2, 2, 4, 16, 128), BF16),
            pltpu.VMEM((4, 16, CH), F32),
            pltpu.VMEM((4, 32, 128), F32),
            pltpu.VMEM((T, CH), F32),
            pltpu.VMEM((T, CH), F32),
            pltpu.VMEM((T, CH), BF16),
            pltpu.VMEM((T, CH), BF16),
            pltpu.VMEM((T, D), F32),
            pltpu.VMEM((8 * T, 128), F32),
            pltpu.VMEM((T, D), BF16),
            pltpu.VMEM((4, npeer, 32, 128), BF16),
            pltpu.VMEM((4, npeer, 32, 128), BF16),
            pltpu.VMEM((T, D), BF16),
            pltpu.VMEM((T, D), F32),
            pltpu.VMEM((T, 3 * D), BF16),
            pltpu.VMEM((T, D), BF16),
            pltpu.VMEM((T, D), BF16),
            pltpu.VMEM((T, 3 * D), BF16),
            pltpu.VMEM((32, 128), F32),
            pltpu.VMEM((256, 128), F32),
            pltpu.VMEM((8, 64, 256), F32),
            dma((4, NCH)),
            dma((2, NCH, 4)),
            dma((2, NCH, 4)),
            dma((2, 2, 4)),
            dma((2, 2, 4)),
            dma((4,)),
            dma((4,)),
            dma((4,)),
        ],
        compiler_params=pltpu.CompilerParams(
            collective_id=0, has_side_effects=True, vmem_limit_bytes=62 * 1024 * 1024
        ),
        cost_estimate=pl.CostEstimate(
            flops=13_000_000_000, bytes_accessed=27_000_000, transcendentals=5_000_000
        ),
    )(
        image,
        gain_conv,
        w_expand,
        kernel_taps,
        w_project,
        gain_attn.reshape(1, D),
        w_qkv,
        bias_table,
        w_out,
        cotangent.reshape(T, D),
    )
    rows = pl.BlockSpec((64, D), lambda i: (i, 0))
    out, dimg = pl.pallas_call(
        last_kernel,
        grid=(T // 64,),
        out_shape=(whole, whole),
        in_specs=[rows, pl.BlockSpec((1, D), lambda i: (0, 0)), rows, rows, rows],
        out_specs=(rows, rows),
    )(image, gain_conv, sent, d_normed, d_mid)
    return out.reshape(height, breadth, width), dimg.reshape(height, breadth, width)


def solution(mesh):
    whole = P("rows", "cols", None)
    return jax.shard_map(
        local,
        mesh=mesh,
        in_specs=(whole, P(), P(), P(), P(), P(), P(), P(), P(), whole),
        out_specs=(whole, whole),
        check_vma=False,
    )
```
